512 devices in a mesh: row: 16 (over z), col: 16 (over x, y_hi, core), rep: 2 (over y_lo).
Axes of the slice: x: 4, y: 4 (y_hi: 2, y_lo: 2; y = y_hi * 2 + y_lo), z: 16, core: 2. Of those that a mesh axis runs over, the one named last changes fastest.
Arguments:
- tokens: bfloat16 [768, 8192], P(('col', 'rep'), 'row'), may hold values from -6 to 6
- cotangent: bfloat16 [768, 8192], P(('col', 'rep'), 'row'), may hold values from -6 to 6
- w1_blocks: bfloat16 [4096, 128, 128], P(('row', 'col')), may hold values from -0.125 to 0.125
- w1_index: int32 [4096, 2], P(('row', 'col')), may hold values from 0 to 15, as said below
- w2_blocks: bfloat16 [4096, 128, 128], P(('row', 'col')), may hold values from -0.0625 to 0.0625
- w2_index: int32 [4096, 2], P(('row', 'col')), may hold values from 0 to 15, as said below
Outputs:
- output: bfloat16 [768, 8192], P(('col', 'rep'), 'row')
- grad_tokens: bfloat16 [768, 8192], P(('col', 'rep'), 'row')
- grad_w1: float32 [4096, 128, 128], P(('row', 'col', 'rep'))
- grad_w2: float32 [4096, 128, 128], P(('row', 'col', 'rep'))
The draws below stay inside these ranges and needn't reach their ends.
Inputs may be any that keep to these rules, and one draw needn't show every extreme that they name: `w1_index`: the 16 pairs (block row, block column) of one tile, entries t * 16 to t * 16 + 15, are distinct; block rows lie below 4, block columns below 16. `w2_index`: the 16 pairs (block row, block column) of one tile, entries t * 16 to t * 16 + 15, are distinct; block rows lie below 16, block columns below 4.
All inputs are finite; a program needn't handle non-finite values.
Results may differ from the reference program's by a relative error of at most 0.018.
Values may be sent and summed in bfloat16 or wider, within the bound.
A program may use at most 64 MiB of HBM per device.

```python
import jax
import jax.numpy as jnp
from jax import lax

D = 8192
FF = 32768
BLOCK = 128
TOK_DEV = 24
TILE_ROWS = 4
TILE_COLS = 16
TILE_BLOCKS = 16
NBLOCKS = 4096
TOKENS = 768
N_ROW = 16
N_COL = 16
N_REP = 2


def draw_w1_index(key, part):
    key = jax.random.fold_in(key, 11)
    tile_keys = jax.random.split(key, N_ROW * N_COL)

    def pick_slots(subkey):
        return jax.random.permutation(subkey, TILE_ROWS * TILE_COLS)[:TILE_BLOCKS]
    chosen = jax.vmap(pick_slots)(tile_keys)
    index_pairs = jnp.stack([chosen // TILE_COLS, chosen % TILE_COLS], axis=-1)
    return index_pairs.reshape(NBLOCKS, 2).astype(jnp.int32)


def draw_w2_index(key, part):
    key = jax.random.fold_in(key, 23)
    tile_keys = jax.random.split(key, N_ROW * N_COL)

    def pick_slots(subkey):
        return jax.random.permutation(subkey, TILE_ROWS * TILE_COLS)[:TILE_BLOCKS]
    chosen = jax.vmap(pick_slots)(tile_keys)
    index_pairs = jnp.stack([chosen // TILE_ROWS, chosen % TILE_ROWS], axis=-1)
    return index_pairs.reshape(NBLOCKS, 2).astype(jnp.int32)


def steps_of(own_key, shape, pieces, low, largest):
    def one(axis_at, shards_of):
        heights = jax.random.uniform(jax.random.fold_in(jax.random.fold_in(own_key, 6), axis_at), (shards_of,), jnp.float32, low / len(pieces), largest / len(pieces))
        return jnp.repeat(jnp.exp(heights), shape[axis_at] // shards_of).reshape((-1,) + (1,) * (len(shape) - axis_at - 1))

    factor_of = one(*pieces[0])
    for cut in pieces[1:]:
        factor_of = factor_of * one(*cut)
    return factor_of


def scatter_about(own_key, extent, scale, most, cuts=(), kind=jnp.bfloat16):
    factor_of = steps_of(own_key, extent, cuts, -0.22, 0.18) if cuts else 1.0
    drawn = jax.random.normal(own_key, extent, jnp.float32) * scale * factor_of
    return jnp.minimum(jnp.maximum(drawn, -most), most).astype(kind)


def setup_inputs(seed: int = 0) -> dict:
    streams_of = jax.random.split(jax.random.key(seed), 7)
    return {
        "tokens": scatter_about(streams_of[0], (TOKENS, D), 1.0, 6.0, ((0, 32), (1, 16))),
        "cotangent": scatter_about(streams_of[1], (TOKENS, D), 1.0, 6.0, ((0, 32), (1, 16))),
        "w1_blocks": scatter_about(streams_of[2], (NBLOCKS, BLOCK, BLOCK), (D // 4) ** -0.5, 0.125, ((0, 256),)),
        "w1_index": draw_w1_index(jax.random.fold_in(streams_of[6], 71), 0),
        "w2_blocks": scatter_about(streams_of[4], (NBLOCKS, BLOCK, BLOCK), (FF // 4) ** -0.5, 0.0625, ((0, 256),)),
        "w2_index": draw_w2_index(jax.random.fold_in(streams_of[6], 71), 0),
    }


def rounded(values):
    return lax.optimization_barrier(values.astype(jnp.bfloat16)).astype(jnp.float32)

def gelu_tanh(values):
    return jax.nn.gelu(values, approximate=True)

def tile_product(panels, blocks, pattern, in_index, out_index, n_in, n_out):
    row_count = panels.shape[0]
    block_size = blocks.shape[-1]
    picked = panels.reshape(row_count, n_in, block_size)[:, in_index, :]
    products = jnp.einsum(pattern, picked.astype(jnp.float32), blocks.astype(jnp.float32))
    onehot = (out_index[:, None] == jnp.arange(n_out, dtype=jnp.int32)[None, :]).astype(jnp.float32)
    result = jnp.einsum('tne,no->toe', products, onehot, precision=lax.Precision.HIGHEST)
    return result.reshape(row_count, n_out * block_size)

def sum_tiles(panels, blocks, index, pattern, in_col, out_col, groups, n_in, n_out):
    token_count = panels.shape[0]
    block_size = blocks.shape[-1]
    width = n_in * block_size

    def one_output(target):

        def add_group(group, total):
            panel_slice = lax.dynamic_slice_in_dim(panels, (group * width).astype(jnp.int32), width, 1)
            tile_blocks = blocks[group, target]
            tile_index = index[group, target]
            product = tile_product(panel_slice, tile_blocks, pattern, tile_index[:, in_col], tile_index[:, out_col], n_in, n_out)
            return total + rounded(product)
        start = jnp.zeros((token_count, n_out * block_size), jnp.float32)
        return lax.fori_loop(jnp.int32(0), jnp.int32(groups), add_group, start)
    result = lax.map(one_output, jnp.arange(blocks.shape[1], dtype=jnp.int32))
    return jnp.transpose(result, (1, 0, 2)).reshape(token_count, -1)

def replica_rows(values):
    width = values.shape[-1]
    return values.reshape(N_COL, N_REP, TOK_DEV, width).transpose(1, 0, 2, 3).reshape(N_REP, N_COL * TOK_DEV, width)

def weight_grads(left, right, index_tiles, left_by_row, n_left, n_right):
    token_count = left.shape[1]

    def per_tile(tile_id):
        row_tile = tile_id // N_COL
        col_tile = tile_id % N_COL
        left_group = row_tile if left_by_row else col_tile
        right_group = col_tile if left_by_row else row_tile
        left_slice = lax.dynamic_slice_in_dim(left, (left_group * n_left * BLOCK).astype(jnp.int32), n_left * BLOCK, 2)
        right_slice = lax.dynamic_slice_in_dim(right, (right_group * n_right * BLOCK).astype(jnp.int32), n_right * BLOCK, 2)
        tile_index = index_tiles[tile_id]
        left_picked = left_slice.reshape(N_REP, token_count, n_left, BLOCK)[:, :, tile_index[:, 0], :]
        right_picked = right_slice.reshape(N_REP, token_count, n_right, BLOCK)[:, :, tile_index[:, 1], :]
        products = jnp.einsum('ptnb,ptne->pnbe', left_picked.astype(jnp.float32), right_picked.astype(jnp.float32))
        return lax.optimization_barrier(jnp.sum(rounded(products), axis=0))
    result = lax.map(per_tile, jnp.arange(N_ROW * N_COL, dtype=jnp.int32))
    return result.reshape(NBLOCKS, BLOCK, BLOCK)

def reference(tokens, cotangent, w1_blocks, w1_index, w2_blocks, w2_index):
    w1_tiles = w1_blocks.reshape(N_ROW, N_COL, TILE_BLOCKS, BLOCK, BLOCK)
    w1_grid = w1_index.reshape(N_ROW, N_COL, TILE_BLOCKS, 2)
    w2_tiles = w2_blocks.reshape(N_ROW, N_COL, TILE_BLOCKS, BLOCK, BLOCK)
    w2_grid = w2_index.reshape(N_ROW, N_COL, TILE_BLOCKS, 2)
    w1_swapped = jnp.transpose(w1_tiles, (1, 0, 2, 3, 4))
    w1_grid_swapped = jnp.transpose(w1_grid, (1, 0, 2, 3))
    w2_swapped = jnp.transpose(w2_tiles, (1, 0, 2, 3, 4))
    w2_grid_swapped = jnp.transpose(w2_grid, (1, 0, 2, 3))
    hidden = sum_tiles(tokens, w1_tiles, w1_grid, 'tnb,nbe->tne', 0, 1, N_ROW, TILE_ROWS, TILE_COLS)
    activated = gelu_tanh(hidden).astype(jnp.bfloat16)
    output = sum_tiles(activated, w2_swapped, w2_grid_swapped, 'tnb,nbe->tne', 0, 1, N_COL, TILE_COLS, TILE_ROWS).astype(jnp.bfloat16)
    grad_act = sum_tiles(cotangent, w2_tiles, w2_grid, 'tnb,neb->tne', 1, 0, N_ROW, TILE_ROWS, TILE_COLS)
    grad_hidden = jax.vjp(gelu_tanh, hidden)[1](grad_act)[0].astype(jnp.bfloat16)
    grad_tokens = sum_tiles(grad_hidden, w1_swapped, w1_grid_swapped, 'tnb,neb->tne', 1, 0, N_COL, TILE_COLS, TILE_ROWS).astype(jnp.bfloat16)
    w1_flat = w1_index.reshape(N_ROW * N_COL, TILE_BLOCKS, 2)
    w2_flat = w2_index.reshape(N_ROW * N_COL, TILE_BLOCKS, 2)
    grad_w1 = weight_grads(replica_rows(tokens), replica_rows(grad_hidden), w1_flat, True, TILE_ROWS, TILE_COLS)
    grad_w2 = weight_grads(replica_rows(activated), replica_rows(cotangent), w2_flat, False, TILE_COLS, TILE_ROWS)
    return (output, grad_tokens, grad_w1, grad_w2)
```

```python
import functools
import math

import jax
import jax.numpy as jnp
from jax import lax
from jax.experimental import pallas as pl
from jax.experimental.pallas import tpu as pltpu
from jax.sharding import PartitionSpec as P

BLK = 128
SUBS = 2
LAG = 2
F32 = jnp.float32
BF16 = jnp.bfloat16
NN = (((1,), (0,)), ((), ()))
NT = (((1,), (1,)), ((), ()))
TN = (((0,), (0,)), ((), ()))
C0 = math.sqrt(2.0 / math.pi)
C1 = 0.044715


def mm(left, right, dims):
    return lax.dot_general(left, right, dims, preferred_element_type=F32)


def stack_blocks(wide, parts):
    return jnp.concatenate([wide[:, a * BLK : (a + 1) * BLK] for a in range(parts)], axis=0)


def widen_blocks(tall, parts):
    rows = tall.shape[0] // parts
    return jnp.concatenate([tall[a * rows : (a + 1) * rows, :] for a in range(parts)], axis=1)


def kernel(
    n_row, n_col, tile_rows, n_blocks, own_blocks, tok_dev,
    tok_ref, cot_ref, inv_ref, idx1_ref, idx2_ref, w1_hbm, w2_hbm,
    out_ref, gt_ref, gw1_ref, gw2_ref,
    w1v, w2v, w1d, w2d, xrecv, xp, xk, part, rs, hid, ag0, ag1, acc, ysend, yrecv, wsend, wown, wrecv,
    load_sem, x_send, x_recv, rs_send, rs_recv, ag_send, ag_recv, y_send, y_recv, w_send, w_recv,
):
    ag = (ag0, ag1)
    z = lax.axis_index("row")
    c = lax.axis_index("col")
    p = lax.axis_index("rep")
    up, down = lax.rem(z + 1, n_row), lax.rem(z + n_row - 1, n_row)
    nxt = (up, down)
    half = n_row // 2
    tokens = tok_dev * n_col
    sub_rows = tokens // SUBS
    fw = tile_rows * BLK

    loads = [
        pltpu.make_async_copy(w1_hbm, w1v.at[pl.ds(0, n_blocks)], load_sem.at[0]),
        pltpu.make_async_copy(w2_hbm, w2v.at[pl.ds(0, n_blocks)], load_sem.at[1]),
    ]
    for load in loads:
        load.start()

    barrier = pltpu.get_barrier_semaphore()

    def greet(off, carry):
        pl.semaphore_signal(barrier, inc=1, device_id={"col": lax.rem(c + off, n_col)})
        return carry

    lax.fori_loop(1, n_col, greet, 0)
    pl.semaphore_signal(barrier, inc=1, device_id={"row": up})
    pl.semaphore_signal(barrier, inc=1, device_id={"row": down})
    pl.semaphore_signal(barrier, inc=1, device_id={"rep": 1 - p})

    for x, ref in enumerate((tok_ref, cot_ref)):
        xrecv[x, c] = stack_blocks(ref[...].astype(F32), tile_rows).astype(BF16)
    pl.semaphore_wait(barrier, n_col - 1 + 3)

    def x_copy(x, off, slot):
        return pltpu.make_async_remote_copy(
            src_ref=xrecv.at[x, slot],
            dst_ref=xrecv.at[x, slot],
            send_sem=x_send.at[x, off],
            recv_sem=x_recv.at[x, off],
            device_id={"col": lax.rem(c + off, n_col)},
        )

    for x in range(2):

        def send_x(off, carry, x=x):
            x_copy(x, off, c).start()
            return carry

        lax.fori_loop(1, n_col, send_x, 0)

    zero_block = jnp.zeros((BLK, BLK), BF16)
    w1v[n_blocks] = zero_block
    w2v[n_blocks] = zero_block
    zeros_half = jnp.zeros((tokens // 2, BLK), BF16)
    for ph in range(2):
        for way in range(2):
            for s_half in range(2):
                is_long = (s_half == 0) == (way == 0)
                rs[ph, way, half if is_long else half - 1, pl.ds(s_half * (tokens // 2), tokens // 2)] = zeros_half
        acc[ph] = jnp.zeros((tokens, fw), F32)
    for load in loads:
        load.wait()

    def dense(j, carry):
        for a in range(tile_rows):
            w1d[j, a * BLK : (a + 1) * BLK, :] = w1v[inv_ref[0, a * n_row + j]]
            w2d[j, :, a * BLK : (a + 1) * BLK] = w2v[inv_ref[1, j * tile_rows + a]]
        return carry

    lax.fori_loop(0, n_row, dense, 0)

    def panel(x):
        def arrive(off, carry):
            x_copy(x, off, lax.rem(c + n_col - off, n_col)).wait_recv()
            return carry

        lax.fori_loop(1, n_col, arrive, 0)
        for m in range(n_col // 2):
            pair = [widen_blocks(xrecv[x, 2 * m + h].astype(F32), tile_rows) for h in range(2)]
            rows = jnp.concatenate(pair, axis=0).astype(BF16)
            span = pl.ds(m * 2 * tok_dev, 2 * tok_dev)
            xp[x, span] = rows
            for a in range(tile_rows):
                xk[x, a, span] = rows[:, a * BLK : (a + 1) * BLK]

    def toward(way, d):
        return lax.rem(z + d, n_row) if way == 0 else lax.rem(z + n_row - d, n_row)

    def long_way(way, s):
        return (s < SUBS // 2) == (way == 0)

    def sub(s):
        return pl.ds(s * sub_rows, sub_rows)

    def product(ph, j):
        if ph == 0:
            return mm(xp[0], w1d[j], NN)
        return mm(xp[1], w2d[j], NT)

    def rs_copy(ph, way, d, s):
        return pltpu.make_async_remote_copy(
            src_ref=rs.at[ph, way, d, sub(s)],
            dst_ref=rs.at[ph, way, d - 1, sub(s)],
            send_sem=rs_send.at[ph, way, d, s],
            recv_sem=rs_recv.at[ph, way, d - 1, s],
            device_id={"row": nxt[way]},
        )

    def rs_terms(ph, d):
        for way in range(2):
            part[ph, way] = product(ph, toward(way, d))

    def rs_pass(ph, d):
        for s in range(SUBS):
            for way in range(2):
                is_long = long_way(way, s)
                last = half if is_long else half - 1

                @pl.when(d <= last)
                def _(s=s, way=way, last=last):
                    @pl.when(d <= last - 1)
                    def _():
                        rs_copy(ph, way, d + 1, s).wait_recv()

                    total = part[ph, way, sub(s)] + rs[ph, way, d, sub(s)].astype(F32)
                    rs[ph, way, d, sub(s)] = total.astype(BF16)
                    rs_copy(ph, way, d, s).start()

    def rs_end(ph):
        part[ph, 0] = product(ph, z)
        for s in range(SUBS):
            for way in range(2):
                rs_copy(ph, way, 1, s).wait_recv()
            total = part[ph, 0, sub(s)] + rs[ph, 0, 0, sub(s)].astype(F32) + rs[ph, 1, 0, sub(s)].astype(F32)
            if ph == 0:
                hid[sub(s)] = total
                tanh = jnp.tanh(C0 * (total + C1 * (total * total * total)))
                value = 0.5 * total * (1.0 + tanh)
            else:
                v = hid[sub(s)]
                tanh = jnp.tanh(C0 * (v + C1 * (v * v * v)))
                slope = 0.5 * (1.0 + tanh) + 0.5 * v * (1.0 - tanh * tanh) * (C0 * (1.0 + 3.0 * C1 * (v * v)))
                value = total * slope
            ag[ph][z, sub(s)] = value.astype(BF16)

    def origin(way, t):
        return lax.rem(z + n_row - t, n_row) if way == 0 else lax.rem(z + t, n_row)

    def ag_copy(ph, way, j, t, s):
        return pltpu.make_async_remote_copy(
            src_ref=ag[ph].at[j, sub(s)],
            dst_ref=ag[ph].at[j, sub(s)],
            send_sem=ag_send.at[ph, way, t, s],
            recv_sem=ag_recv.at[ph, way, t, s],
            device_id={"row": nxt[way]},
        )

    def ag_pass(ph, t):
        for s in range(SUBS):
            for way in range(2):
                hops = half if long_way(way, s) else half - 1
                j = origin(way, t)

                @pl.when((t >= 1) & (t <= hops))
                def _(s=s, way=way, j=j):
                    ag_copy(ph, way, j, t - 1, s).wait_recv()

                @pl.when(t <= hops - 1)
                def _(s=s, way=way, j=j):
                    ag_copy(ph, way, j, t, s).start()

    def consume(ph, j):
        if ph == 0:
            acc[0] += mm(ag0[j], w2d[j], NN)
        else:
            acc[1] += mm(ag1[j], w1d[j], NT)

    def ag_use(ph, t):
        consume(ph, origin(0, t))

        @pl.when((t >= 1) & (t <= half - 1))
        def _():
            consume(ph, origin(1, t))

    def item(i, phases):
        for ph in phases:
            n = i - LAG * ph

            @pl.when(n < half)
            def _(ph=ph, n=n):
                rs_terms(ph, half - n)
                rs_pass(ph, half - n)

            @pl.when(n == half)
            def _(ph=ph, n=n):
                rs_end(ph)

            @pl.when(n > half)
            def _(ph=ph, n=n):
                ag_pass(ph, n - half - 1)

        for ph in phases:
            n = i - LAG * ph

            @pl.when((n > half) & (n <= 2 * half + 1))
            def _(ph=ph, n=n):
                ag_use(ph, n - half - 1)

    panel(0)

    def first(i, carry):
        item(i, (0,))
        return carry

    lax.fori_loop(0, LAG, first, 0)
    panel(1)

    def both(i, carry):
        item(i, (0, 1))
        return carry

    lax.fori_loop(LAG, 2 * half + 1 + LAG, both, 0)

    def y_copy(ph, off, src_slot, dst_slot):
        return pltpu.make_async_remote_copy(
            src_ref=ysend.at[ph, src_slot],
            dst_ref=yrecv.at[ph, dst_slot],
            send_sem=y_send.at[ph, off],
            recv_sem=y_recv.at[ph, off],
            device_id={"col": lax.rem(c + off, n_col)},
        )

    def packed(ph, at):
        rows = acc[ph, pl.ds(pl.multiple_of(at * tok_dev, 8), tok_dev), :]
        return stack_blocks(rows, tile_rows).astype(BF16)

    def send_terms(ph):
        def one(off, carry):
            at = lax.rem(c + off, n_col)
            ysend[ph, at] = packed(ph, at)
            y_copy(ph, off, at, c).start()
            return carry

        lax.fori_loop(1, n_col, one, 0)
        yrecv[ph, c] = packed(ph, c)

    def sum_terms(ph, ref):
        def one(off, carry):
            at = lax.rem(c + n_col - off, n_col)
            y_copy(ph, off, at, at).wait_recv()
            return carry + yrecv[ph, at].astype(F32)

        total = lax.fori_loop(1, n_col, one, yrecv[ph, c].astype(F32))
        ref[...] = widen_blocks(total, tile_rows).astype(BF16)

    def w_copy(ph, m):
        return pltpu.make_async_remote_copy(
            src_ref=wsend.at[ph, m],
            dst_ref=wrecv.at[ph, m],
            send_sem=w_send.at[ph, m],
            recv_sem=w_recv.at[ph, m],
            device_id={"rep": 1 - p},
        )

    def weight_block(ph, n):
        if ph == 0:
            return mm(ag0[idx2_ref[n, 0]], xk[1, idx2_ref[n, 1]], TN)
        return mm(xk[0, idx1_ref[n, 0]], ag1[idx1_ref[n, 1]], TN)

    def send_weights(ph):
        def one(m, carry):
            wsend[ph, m] = weight_block(ph, (1 - p) * own_blocks + m).astype(BF16)
            w_copy(ph, m).start()
            return carry

        lax.fori_loop(0, own_blocks, one, 0)

    def own_weights(ph):
        def one(m, carry):
            wown[ph, m] = weight_block(ph, p * own_blocks + m).astype(BF16)
            return carry

        lax.fori_loop(0, own_blocks, one, 0)

    def sum_weights(ph, ref):
        def one(m, carry):
            w_copy(ph, m).wait_recv()
            ref[m] = wown[ph, m].astype(F32) + wrecv[ph, m].astype(F32)
            return carry

        lax.fori_loop(0, own_blocks, one, 0)

    send_terms(0)
    send_weights(0)
    ag_pass(1, half)
    ag_use(1, half)
    send_weights(1)
    send_terms(1)
    own_weights(0)
    own_weights(1)
    sum_terms(0, out_ref)
    sum_weights(0, gw2_ref)
    sum_terms(1, gt_ref)
    sum_weights(1, gw1_ref)

    for ph in range(2):

        def sent_cols(off, carry, ph=ph):
            x_copy(ph, off, c).wait_send()
            y_copy(ph, off, c, c).wait_send()
            return carry

        lax.fori_loop(1, n_col, sent_cols, 0)

        def sent_weights(m, carry, ph=ph):
            w_copy(ph, m).wait_send()
            return carry

        lax.fori_loop(0, own_blocks, sent_weights, 0)
        for way in range(2):
            for s in range(SUBS):
                hops = half if long_way(way, s) else half - 1

                def sent_rows(t, carry, ph=ph, way=way, s=s):
                    rs_copy(ph, way, t + 1, s).wait_send()
                    ag_copy(ph, way, z, t, s).wait_send()
                    return carry

                lax.fori_loop(0, hops, sent_rows, 0)


def inverse(keys, slots):
    count = keys.shape[0]
    number = jnp.arange(count, dtype=jnp.int32)
    hit = keys[:, None] == jnp.arange(slots, dtype=jnp.int32)[None, :]
    return count + jnp.sum(jnp.where(hit, number[:, None] - count, 0), axis=0)


def shards(n_row, n_col, tokens, cotangent, w1_blocks, w1_index, w2_blocks, w2_index):
    tok_dev, fw = tokens.shape
    tile_rows = fw // BLK
    n_blocks = w1_blocks.shape[0]
    own_blocks = n_blocks // 2
    half = n_row // 2
    toks = tok_dev * n_col
    slots = n_row * tile_rows
    inv = jnp.stack(
        [
            inverse(w1_index[:, 0] * n_row + w1_index[:, 1], slots),
            inverse(w2_index[:, 0] * tile_rows + w2_index[:, 1], slots),
        ]
    )
    vmem = pl.BlockSpec(memory_space=pltpu.VMEM)
    smem = pl.BlockSpec(memory_space=pltpu.SMEM)
    hbm = pl.BlockSpec(memory_space=pl.ANY)
    dma = pltpu.SemaphoreType.DMA
    return pl.pallas_call(
        functools.partial(kernel, n_row, n_col, tile_rows, n_blocks, own_blocks, tok_dev),
        out_shape=(
            jax.ShapeDtypeStruct((tok_dev, fw), BF16),
            jax.ShapeDtypeStruct((tok_dev, fw), BF16),
            jax.ShapeDtypeStruct((own_blocks, BLK, BLK), F32),
            jax.ShapeDtypeStruct((own_blocks, BLK, BLK), F32),
        ),
        in_specs=[vmem, vmem, smem, smem, smem, hbm, hbm],
        out_specs=[vmem] * 4,
        scratch_shapes=[
            pltpu.VMEM((n_blocks + 1, BLK, BLK), BF16),
            pltpu.VMEM((n_blocks + 1, BLK, BLK), BF16),
            pltpu.VMEM((n_row, fw, BLK), BF16),
            pltpu.VMEM((n_row, BLK, fw), BF16),
            pltpu.VMEM((2, n_col, tok_dev * tile_rows, BLK), BF16),
            pltpu.VMEM((2, toks, fw), BF16),
            pltpu.VMEM((2, tile_rows, toks, BLK), BF16),
            pltpu.VMEM((2, 2, toks, BLK), F32),
            pltpu.VMEM((2, 2, half + 1, toks, BLK), BF16),
            pltpu.VMEM((toks, BLK), F32),
            pltpu.VMEM((n_row, toks, BLK), BF16),
            pltpu.VMEM((n_row, toks, BLK), BF16),
            pltpu.VMEM((2, toks, fw), F32),
            pltpu.VMEM((2, n_col, tok_dev * tile_rows, BLK), BF16),
            pltpu.VMEM((2, n_col, tok_dev * tile_rows, BLK), BF16),
            pltpu.VMEM((2, own_blocks, BLK, BLK), BF16),
            pltpu.VMEM((2, own_blocks, BLK, BLK), BF16),
            pltpu.VMEM((2, own_blocks, BLK, BLK), BF16),
            dma((2,)),
            dma((2, n_col)),
            dma((2, n_col)),
            dma((2, 2, half + 1, SUBS)),
            dma((2, 2, half, SUBS)),
            dma((2, 2, half, SUBS)),
            dma((2, 2, half, SUBS)),
            dma((2, n_col)),
            dma((2, n_col)),
            dma((2, own_blocks)),
            dma((2, own_blocks)),
        ],
        compiler_params=pltpu.CompilerParams(
            collective_id=0, has_side_effects=True, vmem_limit_bytes=44 * 1024 * 1024
        ),
        name="ffn",
    )(tokens, cotangent, inv, w1_index, w2_index, w1_blocks, w2_blocks)


def solution(mesh):
    return jax.shard_map(
        functools.partial(shards, mesh.shape["row"], mesh.shape["col"]),
        mesh=mesh,
        in_specs=(
            P(("col", "rep"), "row"),
            P(("col", "rep"), "row"),
            P(("row", "col"), None, None),
            P(("row", "col"), None),
            P(("row", "col"), None, None),
            P(("row", "col"), None),
        ),
        out_specs=(
            P(("col", "rep"), "row"),
            P(("col", "rep"), "row"),
            P(("row", "col", "rep"), None, None),
            P(("row", "col", "rep"), None, None),
        ),
        check_vma=False,
    )
```

```python
import functools
import math

import jax
import jax.numpy as jnp
from jax import lax
from jax.experimental import pallas as pl
from jax.experimental.pallas import tpu as pltpu
from jax.sharding import PartitionSpec as P

BLK = 128
SUBS = 2
LAG = 2
F32 = jnp.float32
BF16 = jnp.bfloat16
NN = (((1,), (0,)), ((), ()))
NT = (((1,), (1,)), ((), ()))
TN = (((0,), (0,)), ((), ()))
C0 = math.sqrt(2.0 / math.pi)
C1 = 0.044715


def mm(left, right, dims):
    return lax.dot_general(left, right, dims, preferred_element_type=F32)


def stack_blocks(wide, parts):
    return jnp.concatenate([wide[:, a * BLK : (a + 1) * BLK] for a in range(parts)], axis=0)


def widen_blocks(tall, parts):
    rows = tall.shape[0] // parts
    return jnp.concatenate([tall[a * rows : (a + 1) * rows, :] for a in range(parts)], axis=1)


def kernel(
    n_row, n_col, tile_rows, n_blocks, own_blocks, tok_dev,
    tok_ref, cot_ref, idx1_hbm, idx2_hbm, w1_hbm, w2_hbm,
    out_ref, gt_ref, gw1_ref, gw2_ref,
    idx1, idx2, w1v, w2v, w1d, w2d, xrecv, xp, xt, part, rs, hid, ag0, ag1, acc, g1d, g2d,
    yown, ys1, yr1, ys2, yr2, ys3, yr3, wsend, wrecv,
    load_sem, x_send, x_recv, rs_send, rs_recv, ag_send, ag_recv, y1_sem, y2_send, y2_recv, y3_sem, w_send, w_recv,
):
    ag = (ag0, ag1)
    z = lax.axis_index("row")
    c = lax.axis_index("col")
    p = lax.axis_index("rep")
    up, down = lax.rem(z + 1, n_row), lax.rem(z + n_row - 1, n_row)
    nxt = (up, down)
    half = n_row // 2
    tokens = tok_dev * n_col
    sub_rows = tokens // SUBS
    fw = tile_rows * BLK
    n_chip = n_col // 2
    n_x = n_col // 4
    col_bits = n_col.bit_length() - 1
    bits = [lax.rem(c // (1 << b), 2) for b in range(col_bits)]
    core, y_hi, x_at = bits[0], bits[1], c // 4

    def flip(q):
        return sum((1 - bits[b] if (q >> b) & 1 else bits[b]) * (1 << b) for b in range(col_bits))

    loads = [
        pltpu.make_async_copy(idx1_hbm, idx1, load_sem.at[0]),
        pltpu.make_async_copy(idx2_hbm, idx2, load_sem.at[1]),
        pltpu.make_async_copy(w1_hbm, w1v.at[pl.ds(0, n_blocks)], load_sem.at[2]),
        pltpu.make_async_copy(w2_hbm, w2v.at[pl.ds(0, n_blocks)], load_sem.at[3]),
    ]
    for load in loads:
        load.start()

    barrier = pltpu.get_barrier_semaphore()
    peers = [flip(q) for q in range(1, n_col)]
    for peer in peers:
        pl.semaphore_signal(barrier, inc=1, device_id={"col": peer})
    pl.semaphore_signal(barrier, inc=1, device_id={"row": up})
    pl.semaphore_signal(barrier, inc=1, device_id={"row": down})
    pl.semaphore_signal(barrier, inc=1, device_id={"rep": 1 - p})

    for x, ref in enumerate((tok_ref, cot_ref)):
        xrecv[x, c] = stack_blocks(ref[...].astype(F32), tile_rows).astype(BF16)
    pl.semaphore_wait(barrier, len(peers) + 3)

    far = [q for q in range(2, n_col, 2) if q & 2] + [q for q in range(2, n_col, 2) if not q & 2]

    def x_copy(x, q, slot):
        return pltpu.make_async_remote_copy(
            src_ref=xrecv.at[x, slot],
            dst_ref=xrecv.at[x, slot],
            send_sem=x_send.at[x, q],
            recv_sem=x_recv.at[x, q],
            device_id={"col": flip(q if x == 0 else (1 if q % 2 else q))},
        )

    def x_start(x):
        for q in (far + [1] if x else far + [q + 1 for q in far] + [1]):
            x_copy(x, q, c).start()

    def x_forward(x):
        for q in (list(reversed(far)) if x else []):
            x_copy(x, q, flip(q)).wait_recv()
            x_copy(x, q + 1, flip(q)).start()

    def panel(x):
        for q in range(1, n_col, 2 if x else 1):
            x_copy(x, q, flip(q)).wait_recv()
        for m in range(n_col // 2):
            pair = [widen_blocks(xrecv[x, 2 * m + h].astype(F32), tile_rows) for h in range(2)]
            xp[x, pl.ds(m * 2 * tok_dev, 2 * tok_dev)] = jnp.concatenate(pair, axis=0).astype(BF16)

    x_start(0)

    zero_block = jnp.zeros((BLK, BLK), BF16)
    w1v[n_blocks] = zero_block
    w2v[n_blocks] = zero_block
    zeros_half = jnp.zeros((tokens // 2, BLK), BF16)
    for ph in range(2):
        for way in range(2):
            for s_half in range(2):
                is_long = (s_half == 0) == (way == 0)
                rs[ph, way, half if is_long else half - 1, pl.ds(s_half * (tokens // 2), tokens // 2)] = zeros_half

    def holder(keys, slot):
        found = jnp.int32(n_blocks)
        for n, key in enumerate(keys):
            found = jnp.where(key == slot, jnp.int32(n), found)
        return found

    def dense1():
        loads[0].wait()
        loads[2].wait()
        keys = [idx1[0, n] * n_row + idx1[1, n] for n in range(n_blocks)]

        def one(j, carry):
            for a in range(tile_rows):
                w1d[j, a * BLK : (a + 1) * BLK, :] = w1v[holder(keys, a * n_row + j)]
            return carry

        lax.fori_loop(0, n_row, one, 0)

    def dense2():
        loads[1].wait()
        loads[3].wait()
        keys = [idx2[0, n] * tile_rows + idx2[1, n] for n in range(n_blocks)]

        def one(j, carry):
            for a in range(tile_rows):
                w2d[j, :, a * BLK : (a + 1) * BLK] = w2v[holder(keys, j * tile_rows + a)]
            return carry

        lax.fori_loop(0, n_row, one, 0)

    def toward(way, d):
        return lax.rem(z + d, n_row) if way == 0 else lax.rem(z + n_row - d, n_row)

    def long_way(way, s):
        return (s < SUBS // 2) == (way == 0)

    def sub(s):
        return pl.ds(s * sub_rows, sub_rows)

    def product(ph, j):
        if ph == 0:
            return mm(xp[0], w1d[j], NN)
        return mm(xp[1], w2d[j], NT)

    def rs_copy(ph, way, d, s):
        return pltpu.make_async_remote_copy(
            src_ref=rs.at[ph, way, d, sub(s)],
            dst_ref=rs.at[ph, way, d - 1, sub(s)],
            send_sem=rs_send.at[ph, way, d, s],
            recv_sem=rs_recv.at[ph, way, d - 1, s],
            device_id={"row": nxt[way]},
        )

    def rs_terms(ph, d):
        for way in range(2):
            part[ph, way] = product(ph, toward(way, d))

    def rs_pass(ph, d):
        for s in range(SUBS):
            for way in range(2):
                is_long = long_way(way, s)
                last = half if is_long else half - 1

                @pl.when(d <= last)
                def _(s=s, way=way, last=last):
                    @pl.when(d <= last - 1)
                    def _():
                        rs_copy(ph, way, d + 1, s).wait_recv()

                    total = part[ph, way, sub(s)] + rs[ph, way, d, sub(s)].astype(F32)
                    rs[ph, way, d, sub(s)] = total.astype(BF16)
                    rs_copy(ph, way, d, s).start()

    def rs_end(ph):
        part[ph, 0] = product(ph, z)
        for s in range(SUBS):
            for way in range(2):
                rs_copy(ph, way, 1, s).wait_recv()
            total = part[ph, 0, sub(s)] + rs[ph, 0, 0, sub(s)].astype(F32) + rs[ph, 1, 0, sub(s)].astype(F32)
            if ph == 0:
                hid[sub(s)] = total
                tanh = jnp.tanh(C0 * (total + C1 * (total * total * total)))
                value = 0.5 * total * (1.0 + tanh)
            else:
                v = hid[sub(s)]
                tanh = jnp.tanh(C0 * (v + C1 * (v * v * v)))
                slope = 0.5 * (1.0 + tanh) + 0.5 * v * (1.0 - tanh * tanh) * (C0 * (1.0 + 3.0 * C1 * (v * v)))
                value = total * slope
            ag[ph][z, sub(s)] = value.astype(BF16)

    def origin(way, t):
        return lax.rem(z + n_row - t, n_row) if way == 0 else lax.rem(z + t, n_row)

    def ag_copy(ph, way, j, t, s):
        return pltpu.make_async_remote_copy(
            src_ref=ag[ph].at[j, sub(s)],
            dst_ref=ag[ph].at[j, sub(s)],
            send_sem=ag_send.at[ph, way, t, s],
            recv_sem=ag_recv.at[ph, way, t, s],
            device_id={"row": nxt[way]},
        )

    def ag_pass(ph, t):
        for s in range(SUBS):
            for way in range(2):
                hops = half if long_way(way, s) else half - 1
                j = origin(way, t)

                @pl.when((t >= 1) & (t <= hops))
                def _(s=s, way=way, j=j):
                    ag_copy(ph, way, j, t - 1, s).wait_recv()

                @pl.when(t <= hops - 1)
                def _(s=s, way=way, j=j):
                    ag_copy(ph, way, j, t, s).start()

    def consume(ph, j):
        if ph == 0:
            acc[0] += mm(ag0[j], w2d[j], NN)
            grad = mm(ag0[j], xp[1], TN)
            for a in range(tile_rows):
                g2d[j, a] = grad[:, a * BLK : (a + 1) * BLK].astype(BF16)
        else:
            acc[1] += mm(ag1[j], w1d[j], NT)
            grad = mm(xt[...], ag1[j], NN)
            for a in range(tile_rows):
                g1d[j, a] = grad[a * BLK : (a + 1) * BLK, :].astype(BF16)

    def ag_use(ph, t):
        consume(ph, origin(0, t))

        @pl.when((t >= 1) & (t <= half - 1))
        def _():
            consume(ph, origin(1, t))

    def item(i, phases):
        for ph in phases:
            n = i - LAG * ph

            @pl.when(n < half)
            def _(ph=ph, n=n):
                rs_terms(ph, half - n)
                rs_pass(ph, half - n)

            @pl.when(n == half)
            def _(ph=ph, n=n):
                rs_end(ph)

            @pl.when(n > half)
            def _(ph=ph, n=n):
                ag_pass(ph, n - half - 1)

        for ph in phases:
            n = i - LAG * ph

            @pl.when((n > half) & (n <= 2 * half + 1))
            def _(ph=ph, n=n):
                ag_use(ph, n - half - 1)

    def packed(ph, at):
        rows = acc[ph, pl.ds(pl.multiple_of(at * tok_dev, 8), tok_dev), :]
        return stack_blocks(rows, tile_rows)

    def y1_copy(ph):
        return pltpu.make_async_remote_copy(
            src_ref=ys1.at[ph],
            dst_ref=yr1.at[ph],
            send_sem=y1_sem.at[0, ph],
            recv_sem=y1_sem.at[1, ph],
            device_id={"col": flip(1)},
        )

    def y2_copy(ph, dx):
        to = flip(4 * dx)
        return pltpu.make_async_remote_copy(
            src_ref=ys2.at[ph, pl.ds(2 * (to // 4), 2)],
            dst_ref=yr2.at[ph, dx - 1],
            send_sem=y2_send.at[ph, dx - 1],
            recv_sem=y2_recv.at[ph, dx - 1],
            device_id={"col": to},
        )

    def y3_copy(ph):
        return pltpu.make_async_remote_copy(
            src_ref=ys3.at[ph],
            dst_ref=yr3.at[ph],
            send_sem=y3_sem.at[0, ph],
            recv_sem=y3_sem.at[1, ph],
            device_id={"col": flip(2)},
        )

    def y1(ph):
        def one(i, carry):
            ys1[ph, i] = packed(ph, 2 * i + 1 - core).astype(BF16)
            return carry

        lax.fori_loop(0, n_chip, one, 0)
        y1_copy(ph).start()

        def own(i, carry):
            yown[ph, i] = packed(ph, 2 * i + core)
            return carry

        lax.fori_loop(0, n_chip, own, 0)

    def y2(ph):
        y1_copy(ph).wait_recv()

        def one(i, carry):
            total = yown[ph, i] + yr1[ph, i].astype(F32)
            yown[ph, i] = total
            ys2[ph, i] = total.astype(BF16)
            return carry

        lax.fori_loop(0, n_chip, one, 0)
        for dx in range(1, n_x):
            y2_copy(ph, dx).start()

    def y3(ph):
        for dx in range(1, n_x):
            y2_copy(ph, dx).wait_recv()

        def summed(at):
            total = yown[ph, 2 * x_at + at]
            for dx in range(1, n_x):
                total += yr2[ph, dx - 1, at].astype(F32)
            return total

        ys3[ph] = summed(1 - y_hi).astype(BF16)
        y3_copy(ph).start()
        yown[ph, 0] = summed(y_hi)

    def y4(ph, ref):
        y3_copy(ph).wait_recv()
        ref[...] = widen_blocks(yown[ph, 0] + yr3[ph].astype(F32), tile_rows).astype(BF16)

    def w_copy(ph, m):
        return pltpu.make_async_remote_copy(
            src_ref=wsend.at[ph, m],
            dst_ref=wrecv.at[ph, m],
            send_sem=w_send.at[ph, m],
            recv_sem=w_recv.at[ph, m],
            device_id={"rep": 1 - p},
        )

    def weight_block(ph, n):
        if ph == 0:
            return g2d[idx2[0, n], idx2[1, n]]
        return g1d[idx1[1, n], idx1[0, n]]

    def send_weights(ph):
        def one(m, carry):
            wsend[ph, m] = weight_block(ph, (1 - p) * own_blocks + m)
            w_copy(ph, m).start()
            return carry

        lax.fori_loop(0, own_blocks, one, 0)

    def sum_weights(ph, ref):
        def one(m, carry):
            w_copy(ph, m).wait_recv()
            ref[m] = weight_block(ph, p * own_blocks + m).astype(F32) + wrecv[ph, m].astype(F32)
            return carry

        lax.fori_loop(0, own_blocks, one, 0)

    dense1()
    x_forward(0)
    x_start(1)
    panel(0)
    item(0, (0,))
    x_forward(1)
    dense2()
    for ph in range(2):
        acc[ph] = jnp.zeros((tokens, fw), F32)
    xt[...] = jnp.transpose(xp[0])

    def first(i, carry):
        item(i, (0,))
        return carry

    lax.fori_loop(1, LAG, first, 0)
    panel(1)

    def both(i, carry):
        item(i, (0, 1))

        @pl.when(i == 2 * half + 1)
        def _():
            y1(0)
            send_weights(0)

        return carry

    lax.fori_loop(LAG, 2 * half + 1 + LAG, both, 0)
    y2(0)
    ag_pass(1, half)
    ag_use(1, half)
    y1(1)
    send_weights(1)
    y3(0)
    y2(1)
    y4(0, out_ref)
    sum_weights(0, gw2_ref)
    y3(1)
    sum_weights(1, gw1_ref)
    y4(1, gt_ref)

    for ph in range(2):
        for q in range(1, n_col):
            x_copy(ph, q, c).wait_send()
        y1_copy(ph).wait_send()
        for dx in range(1, n_x):
            y2_copy(ph, dx).wait_send()
        y3_copy(ph).wait_send()

        def sent_weights(m, carry, ph=ph):
            w_copy(ph, m).wait_send()
            return carry

        lax.fori_loop(0, own_blocks, sent_weights, 0)
        for way in range(2):
            for s in range(SUBS):
                hops = half if long_way(way, s) else half - 1

                def sent_rows(t, carry, ph=ph, way=way, s=s):
                    rs_copy(ph, way, t + 1, s).wait_send()
                    ag_copy(ph, way, z, t, s).wait_send()
                    return carry

                lax.fori_loop(0, hops, sent_rows, 0)


def shards(n_row, n_col, tokens, cotangent, w1_blocks, w1_index, w2_blocks, w2_index):
    tok_dev, fw = tokens.shape
    tile_rows = fw // BLK
    n_blocks = w1_blocks.shape[0]
    own_blocks = n_blocks // 2
    half = n_row // 2
    toks = tok_dev * n_col
    n_chip = n_col // 2
    n_x = n_col // 4
    piece = (tok_dev * tile_rows, BLK)
    vmem = pl.BlockSpec(memory_space=pltpu.VMEM)
    hbm = pl.BlockSpec(memory_space=pltpu.HBM)
    dma = pltpu.SemaphoreType.DMA
    shapes = (
        pltpu.VMEM((tok_dev, fw), BF16),
        pltpu.VMEM((tok_dev, fw), BF16),
        pltpu.VMEM((own_blocks, BLK, BLK), F32),
        pltpu.VMEM((own_blocks, BLK, BLK), F32),
    )
    operands = [
        pltpu.with_memory_space_constraint(array, pltpu.HBM)
        for array in (tokens, cotangent, w1_index.T, w2_index.T, w1_blocks, w2_blocks)
    ]
    return pl.pallas_call(
        functools.partial(kernel, n_row, n_col, tile_rows, n_blocks, own_blocks, tok_dev),
        out_shape=shapes,
        in_specs=[vmem, vmem, hbm, hbm, hbm, hbm],
        out_specs=[vmem] * 4,
        scratch_shapes=[
            pltpu.SMEM((2, n_blocks), jnp.int32),
            pltpu.SMEM((2, n_blocks), jnp.int32),
            pltpu.VMEM((n_blocks + 1, BLK, BLK), BF16),
            pltpu.VMEM((n_blocks + 1, BLK, BLK), BF16),
            pltpu.VMEM((n_row, fw, BLK), BF16),
            pltpu.VMEM((n_row, BLK, fw), BF16),
            pltpu.VMEM((2, n_col) + piece, BF16),
            pltpu.VMEM((2, toks, fw), BF16),
            pltpu.VMEM((fw, toks), BF16),
            pltpu.VMEM((2, 2, toks, BLK), F32),
            pltpu.VMEM((2, 2, half + 1, toks, BLK), BF16),
            pltpu.VMEM((toks, BLK), F32),
            pltpu.VMEM((n_row, toks, BLK), BF16),
            pltpu.VMEM((n_row, toks, BLK), BF16),
            pltpu.VMEM((2, toks, fw), F32),
            pltpu.VMEM((n_row, tile_rows, BLK, BLK), BF16),
            pltpu.VMEM((n_row, tile_rows, BLK, BLK), BF16),
            pltpu.VMEM((2, n_chip) + piece, F32),
            pltpu.VMEM((2, n_chip) + piece, BF16),
            pltpu.VMEM((2, n_chip) + piece, BF16),
            pltpu.VMEM((2, n_chip) + piece, BF16),
            pltpu.VMEM((2, max(n_x - 1, 1), 2) + piece, BF16),
            pltpu.VMEM((2,) + piece, BF16),
            pltpu.VMEM((2,) + piece, BF16),
            pltpu.VMEM((2, own_blocks, BLK, BLK), BF16),
            pltpu.VMEM((2, own_blocks, BLK, BLK), BF16),
            dma((4,)),
            dma((2, n_col)),
            dma((2, n_col)),
            dma((2, 2, half + 1, SUBS)),
            dma((2, 2, half, SUBS)),
            dma((2, 2, half, SUBS)),
            dma((2, 2, half, SUBS)),
            dma((2, 2)),
            dma((2, max(n_x - 1, 1))),
            dma((2, max(n_x - 1, 1))),
            dma((2, 2)),
            dma((2, own_blocks)),
            dma((2, own_blocks)),
        ],
        compiler_params=pltpu.CompilerParams(
            collective_id=0, has_side_effects=True, vmem_limit_bytes=44 * 1024 * 1024
        ),
        name="ffn",
    )(*operands)


def solution(mesh):
    return jax.shard_map(
        functools.partial(shards, mesh.shape["row"], mesh.shape["col"]),
        mesh=mesh,
        in_specs=(
            P(("col", "rep"), "row"),
            P(("col", "rep"), "row"),
            P(("row", "col"), None, None),
            P(("row", "col"), None),
            P(("row", "col"), None, None),
            P(("row", "col"), None),
        ),
        out_specs=(
            P(("col", "rep"), "row"),
            P(("col", "rep"), "row"),
            P(("row", "col", "rep"), None, None),
            P(("row", "col", "rep"), None, None),
        ),
        check_vma=False,
    )
```

```python
import functools
import math

import jax
import jax.numpy as jnp
from jax import lax
from jax.experimental import pallas as pl
from jax.experimental.pallas import tpu as pltpu
from jax.sharding import PartitionSpec as P

BLK = 128
SUBS = 2
LAG = 2
F32 = jnp.float32
BF16 = jnp.bfloat16
NN = (((1,), (0,)), ((), ()))
NT = (((1,), (1,)), ((), ()))
TN = (((0,), (0,)), ((), ()))
C0 = math.sqrt(2.0 / math.pi)
C1 = 0.044715


def mm(left, right, dims):
    return lax.dot_general(left, right, dims, preferred_element_type=F32)


def stack_blocks(wide, parts):
    return jnp.concatenate([wide[:, a * BLK : (a + 1) * BLK] for a in range(parts)], axis=0)


def widen_blocks(tall, parts):
    rows = tall.shape[0] // parts
    return jnp.concatenate([tall[a * rows : (a + 1) * rows, :] for a in range(parts)], axis=1)


def kernel(
    n_row, n_col, tile_rows, n_blocks, own_blocks, tok_dev,
    tok_ref, cot_ref, idx1_hbm, idx2_hbm, w1_hbm, w2_hbm,
    out_ref, gt_ref, gw1_ref, gw2_ref,
    idx1, idx2, w1v, w2v, w1d, w2d, xrecv, xp, xt, part, rs, hid, ag0, ag1, acc, g1d, g2d,
    yown, ylast, ys1, yr1, ys2, yr2, ys3, yr3, wsend, wrecv,
    load_sem, x_send, x_recv, rs_send, rs_recv, ag_send, ag_recv, y1_send, y1_recv, y2_send, y2_recv, y3_sem, w_send, w_recv,
):
    ag = (ag0, ag1)
    z = lax.axis_index("row")
    c = lax.axis_index("col")
    p = lax.axis_index("rep")
    up, down = lax.rem(z + 1, n_row), lax.rem(z + n_row - 1, n_row)
    nxt = (up, down)
    half = n_row // 2
    tokens = tok_dev * n_col
    sub_rows = tokens // SUBS
    fw = tile_rows * BLK
    n_x = n_col // 4
    col_bits = n_col.bit_length() - 1
    bits = [lax.rem(c // (1 << b), 2) for b in range(col_bits)]
    core, y_hi = bits[0], bits[1]

    def flip(q):
        return sum((1 - bits[b] if (q >> b) & 1 else bits[b]) * (1 << b) for b in range(col_bits))

    own_place = 2 * (c // 4) + core

    loads = [
        pltpu.make_async_copy(idx1_hbm, idx1, load_sem.at[0]),
        pltpu.make_async_copy(idx2_hbm, idx2, load_sem.at[1]),
        pltpu.make_async_copy(w1_hbm, w1v.at[pl.ds(0, n_blocks)], load_sem.at[2]),
        pltpu.make_async_copy(w2_hbm, w2v.at[pl.ds(0, n_blocks)], load_sem.at[3]),
    ]
    for load in loads:
        load.start()

    barrier = pltpu.get_barrier_semaphore()
    peers = [flip(q) for q in range(1, n_col)]
    for peer in peers:
        pl.semaphore_signal(barrier, inc=1, device_id={"col": peer})
    pl.semaphore_signal(barrier, inc=1, device_id={"row": up})
    pl.semaphore_signal(barrier, inc=1, device_id={"row": down})
    pl.semaphore_signal(barrier, inc=1, device_id={"rep": 1 - p})

    for x, ref in enumerate((tok_ref, cot_ref)):
        xrecv[x, own_place] = stack_blocks(ref[...].astype(F32), tile_rows).astype(BF16)
    pl.semaphore_wait(barrier, len(peers) + 3)

    near = [q for q in range(1, n_col) if not q & 2]
    far = [q for q in range(1, n_col) if q & 2]
    even = [q for q in far + near if q % 2 == 0]

    def place(q):
        return (q >> 1 & 1) * (n_col // 2) + 2 * (flip(q) // 4) + (1 - core if q % 2 else core)

    def x_copy(x, q, direct=True):
        source = place(0) if direct else place(q)
        return pltpu.make_async_remote_copy(
            src_ref=xrecv.at[x, source],
            dst_ref=xrecv.at[x, (q >> 1 & 1) * (n_col // 2) + place(0) if direct else place(q)],
            send_sem=x_send.at[x, q],
            recv_sem=x_recv.at[x, q],
            device_id={"col": flip(q if x == 0 else (1 if q % 2 else q))},
        )

    def x_arrive(x, q):
        x_copy(x, q, False).wait_recv()

    def x_start(x):
        for q in even + [1] if x else near + far:
            x_copy(x, q).start()

    def x_forward(x):
        for q in reversed(even):
            x_arrive(x, q)
            pltpu.make_async_remote_copy(
                src_ref=xrecv.at[x, place(q)],
                dst_ref=xrecv.at[x, place(q)],
                send_sem=x_send.at[x, q + 1],
                recv_sem=x_recv.at[x, q + 1],
                device_id={"col": flip(1)},
            ).start()

    def panel(x, part_no):
        for q in (near, far)[part_no]:
            if x == 0 or q % 2:
                x_arrive(x, q)
        for m in range(n_col // 4):
            at = part_no * (n_col // 2) + 2 * m
            pair = [widen_blocks(xrecv[x, at + h].astype(F32), tile_rows) for h in range(2)]
            xp[x, pl.ds(at * tok_dev, 2 * tok_dev)] = jnp.concatenate(pair, axis=0).astype(BF16)

    x_start(0)

    zero_block = jnp.zeros((BLK, BLK), BF16)
    w1v[n_blocks] = zero_block
    w2v[n_blocks] = zero_block
    zeros_half = jnp.zeros((tokens // 2, BLK), BF16)
    for ph in range(2):
        for way in range(2):
            for s_half in range(2):
                is_long = (s_half == 0) == (way == 0)
                rs[ph, way, half if is_long else half - 1, pl.ds(s_half * (tokens // 2), tokens // 2)] = zeros_half

    def holder(keys, slot):
        found = jnp.int32(n_blocks)
        for n, key in enumerate(keys):
            found = jnp.where(key == slot, jnp.int32(n), found)
        return found

    def dense1():
        loads[0].wait()
        loads[2].wait()
        keys = [idx1[0, n] * n_row + idx1[1, n] for n in range(n_blocks)]

        def one(j, carry):
            for a in range(tile_rows):
                w1d[j, a * BLK : (a + 1) * BLK, :] = w1v[holder(keys, a * n_row + j)]
            return carry

        lax.fori_loop(0, n_row, one, 0)

    def dense2():
        loads[1].wait()
        loads[3].wait()
        keys = [idx2[0, n] * tile_rows + idx2[1, n] for n in range(n_blocks)]

        def one(j, carry):
            for a in range(tile_rows):
                w2d[j, :, a * BLK : (a + 1) * BLK] = w2v[holder(keys, j * tile_rows + a)]
            return carry

        lax.fori_loop(0, n_row, one, 0)

    def toward(way, d):
        return lax.rem(z + d, n_row) if way == 0 else lax.rem(z + n_row - d, n_row)

    def long_way(way, s):
        return (s < SUBS // 2) == (way == 0)

    def sub(s):
        return pl.ds(s * sub_rows, sub_rows)

    def product(ph, j, rows):
        if ph == 0:
            return mm(xp[0, rows], w1d[j], NN)
        return mm(xp[1, rows], w2d[j], NT)

    def rs_copy(ph, way, d, s):
        return pltpu.make_async_remote_copy(
            src_ref=rs.at[ph, way, d, sub(s)],
            dst_ref=rs.at[ph, way, d - 1, sub(s)],
            send_sem=rs_send.at[ph, way, d, s],
            recv_sem=rs_recv.at[ph, way, d - 1, s],
            device_id={"row": nxt[way]},
        )

    def rs_terms(ph, n, subs):
        for s in subs:
            for way in range(2):
                d = (half if long_way(way, s) else half - 1) - n

                @pl.when(d >= 1)
                def _(s=s, way=way, d=d):
                    part[ph, way, sub(s)] = product(ph, toward(way, d), sub(s))

    def rs_pass(ph, n, subs):
        for s in subs:
            for way in range(2):
                d = (half if long_way(way, s) else half - 1) - n

                @pl.when(d >= 1)
                def _(s=s, way=way, d=d):
                    @pl.when(n >= 1)
                    def _():
                        rs_copy(ph, way, d + 1, s).wait_recv()

                    total = part[ph, way, sub(s)] + rs[ph, way, d, sub(s)].astype(F32)
                    rs[ph, way, d, sub(s)] = total.astype(BF16)
                    rs_copy(ph, way, d, s).start()

    def rs_end(ph):
        for s in range(SUBS):
            part[ph, 0, sub(s)] = product(ph, z, sub(s))
        for s in range(SUBS):
            for way in range(2):
                rs_copy(ph, way, 1, s).wait_recv()
            total = part[ph, 0, sub(s)] + rs[ph, 0, 0, sub(s)].astype(F32) + rs[ph, 1, 0, sub(s)].astype(F32)
            if ph == 0:
                hid[sub(s)] = total
                tanh = jnp.tanh(C0 * (total + C1 * (total * total * total)))
                value = 0.5 * total * (1.0 + tanh)
            else:
                v = hid[sub(s)]
                tanh = jnp.tanh(C0 * (v + C1 * (v * v * v)))
                slope = 0.5 * (1.0 + tanh) + 0.5 * v * (1.0 - tanh * tanh) * (C0 * (1.0 + 3.0 * C1 * (v * v)))
                value = total * slope
            ag[ph][z, sub(s)] = value.astype(BF16)
            for way in range(2):
                ag_copy(ph, way, z, 0, s).start()

    def origin(way, t):
        return lax.rem(z + n_row - t, n_row) if way == 0 else lax.rem(z + t, n_row)

    def ag_copy(ph, way, j, t, s):
        return pltpu.make_async_remote_copy(
            src_ref=ag[ph].at[j, sub(s)],
            dst_ref=ag[ph].at[j, sub(s)],
            send_sem=ag_send.at[ph, way, t, s],
            recv_sem=ag_recv.at[ph, way, t, s],
            device_id={"row": nxt[way]},
        )

    def ag_pass(ph, t):
        for s in range(SUBS):
            for way in range(2):
                hops = half if long_way(way, s) else half - 1
                j = origin(way, t)

                @pl.when(t <= hops)
                def _(s=s, way=way, j=j):
                    ag_copy(ph, way, j, t - 1, s).wait_recv()

                @pl.when(t <= hops - 1)
                def _(s=s, way=way, j=j):
                    ag_copy(ph, way, j, t, s).start()

    def consume(ph, j):
        if ph == 0:
            acc[0] += mm(ag0[j], w2d[j], NN)
            grad = mm(ag0[j], xp[1], TN)
            for a in range(tile_rows):
                g2d[j, a] = grad[:, a * BLK : (a + 1) * BLK].astype(BF16)
        else:
            acc[1] += mm(ag1[j], w1d[j], NT)
            grad = mm(xt[...], ag1[j], NN)
            for a in range(tile_rows):
                g1d[j, a] = grad[a * BLK : (a + 1) * BLK, :].astype(BF16)

    def ag_use(ph, t):
        consume(ph, origin(0, t))

        @pl.when((t >= 1) & (t <= half - 1))
        def _():
            consume(ph, origin(1, t))

    def item(i, phases):
        for ph in phases:
            n = i - LAG * ph

            @pl.when(n < half)
            def _(ph=ph, n=n):
                rs_terms(ph, n, range(SUBS))
                rs_pass(ph, n, range(SUBS))

            @pl.when(n == half)
            def _(ph=ph):
                rs_end(ph)

            @pl.when(n > half)
            def _(ph=ph, n=n):
                ag_pass(ph, n - half)

        for ph in phases:
            n = i - LAG * ph

            @pl.when((n >= half) & (n <= 2 * half))
            def _(ph=ph, n=n):
                ag_use(ph, n - half)

    def packed(ph, at):
        rows = acc[ph, pl.ds(pl.multiple_of(at * tok_dev, 8), tok_dev), :]
        return stack_blocks(rows, tile_rows)

    def y1_copy(ph, dx):
        at = 2 * (flip(4 * dx) // 4)
        return pltpu.make_async_remote_copy(
            src_ref=ys1.at[ph, pl.ds(at, 2)],
            dst_ref=yr1.at[ph, pl.ds(at, 2)],
            send_sem=y1_send.at[ph, dx],
            recv_sem=y1_recv.at[ph, dx],
            device_id={"col": flip(1)},
        )

    def y2_copy(ph, dx):
        to = flip(4 * dx)
        return pltpu.make_async_remote_copy(
            src_ref=ys2.at[ph, pl.ds(2 * (to // 4), 2)],
            dst_ref=yr2.at[ph, dx - 1],
            send_sem=y2_send.at[ph, dx - 1],
            recv_sem=y2_recv.at[ph, dx - 1],
            device_id={"col": to},
        )

    def y3_copy(ph):
        return pltpu.make_async_remote_copy(
            src_ref=ys3.at[ph],
            dst_ref=yr3.at[ph],
            send_sem=y3_sem.at[0, ph],
            recv_sem=y3_sem.at[1, ph],
            device_id={"col": flip(2)},
        )

    x_order = sorted(range(n_x), key=lambda dx: (dx == 0, dx != 2))

    def y1(ph):
        for dx in x_order:
            at = 2 * (flip(4 * dx) // 4)
            for y in range(2):
                ys1[ph, at + y] = packed(ph, lax.rem(y + y_hi, 2) * (n_col // 2) + at + 1 - core).astype(BF16)
            y1_copy(ph, dx).start()

    def y2(ph):
        for dx in x_order:
            at = 2 * (flip(4 * dx) // 4)
            own = [packed(ph, lax.rem(y + y_hi, 2) * (n_col // 2) + at + core) for y in range(2)]
            y1_copy(ph, dx).wait_recv()
            for y in range(2):
                total = own[y] + yr1[ph, at + y].astype(F32)
                if dx:
                    ys2[ph, at + y] = total.astype(BF16)
                else:
                    yown[ph, y] = total
            if dx:
                y2_copy(ph, dx).start()

    def y3(ph):
        for dx in range(1, n_x):
            y2_copy(ph, dx).wait_recv()

        def summed(at):
            total = yown[ph, at]
            for dx in range(1, n_x):
                total += yr2[ph, dx - 1, at].astype(F32)
            return total

        ys3[ph] = summed(1 - y_hi).astype(BF16)
        y3_copy(ph).start()
        ylast[ph] = summed(y_hi)

    def y4(ph, ref):
        y3_copy(ph).wait_recv()
        ref[...] = widen_blocks(ylast[ph] + yr3[ph].astype(F32), tile_rows).astype(BF16)

    def w_copy(ph, m):
        return pltpu.make_async_remote_copy(
            src_ref=wsend.at[ph, m],
            dst_ref=wrecv.at[ph, m],
            send_sem=w_send.at[ph, m],
            recv_sem=w_recv.at[ph, m],
            device_id={"rep": 1 - p},
        )

    def weight_block(ph, n):
        if ph == 0:
            return g2d[idx2[0, n], idx2[1, n]]
        return g1d[idx1[1, n], idx1[0, n]]

    def send_weights(ph):
        def one(m, carry):
            wsend[ph, m] = weight_block(ph, (1 - p) * own_blocks + m)
            w_copy(ph, m).start()
            return carry

        lax.fori_loop(0, own_blocks, one, 0)

    def sum_weights(ph, ref):
        def one(m, carry):
            w_copy(ph, m).wait_recv()
            ref[m] = weight_block(ph, p * own_blocks + m).astype(F32) + wrecv[ph, m].astype(F32)
            return carry

        lax.fori_loop(0, own_blocks, one, 0)

    dense1()
    x_start(1)
    for s in range(SUBS):
        panel(0, s)
        rs_terms(0, 0, (s,))
        rs_pass(0, 0, (s,))
    dense2()
    for ph in range(2):
        acc[ph] = jnp.zeros((tokens, fw), F32)

    def first(i, carry):
        item(i, (0,))
        return carry

    lax.fori_loop(1, LAG, first, 0)
    x_forward(1)
    xt[...] = jnp.transpose(xp[0])
    panel(1, 0)
    panel(1, 1)

    def both(i, carry):
        item(i, (0, 1))

        @pl.when(i == 2 * half)
        def _():
            y1(0)
            send_weights(0)

        return carry

    lax.fori_loop(LAG, 2 * half + LAG, both, 0)
    y2(0)
    ag_pass(1, half)
    ag_use(1, half)
    y1(1)
    send_weights(1)
    y3(0)
    y2(1)
    y4(0, out_ref)
    sum_weights(0, gw2_ref)
    y3(1)
    sum_weights(1, gw1_ref)
    y4(1, gt_ref)

    for ph in range(2):
        for q in range(1, n_col):
            x_copy(ph, q).wait_send()
        for dx in range(n_x):
            y1_copy(ph, dx).wait_send()
        for dx in range(1, n_x):
            y2_copy(ph, dx).wait_send()
        y3_copy(ph).wait_send()

        def sent_weights(m, carry, ph=ph):
            w_copy(ph, m).wait_send()
            return carry

        lax.fori_loop(0, own_blocks, sent_weights, 0)
        for way in range(2):
            for s in range(SUBS):
                hops = half if long_way(way, s) else half - 1

                def sent_rows(t, carry, ph=ph, way=way, s=s):
                    rs_copy(ph, way, t + 1, s).wait_send()
                    ag_copy(ph, way, z, t, s).wait_send()
                    return carry

                lax.fori_loop(0, hops, sent_rows, 0)


def shards(n_row, n_col, tokens, cotangent, w1_blocks, w1_index, w2_blocks, w2_index):
    tok_dev, fw = tokens.shape
    tile_rows = fw // BLK
    n_blocks = w1_blocks.shape[0]
    own_blocks = n_blocks // 2
    half = n_row // 2
    toks = tok_dev * n_col
    n_chip = n_col // 2
    n_x = n_col // 4
    piece = (tok_dev * tile_rows, BLK)
    vmem = pl.BlockSpec(memory_space=pltpu.VMEM)
    hbm = pl.BlockSpec(memory_space=pltpu.HBM)
    dma = pltpu.SemaphoreType.DMA
    shapes = (
        pltpu.VMEM((tok_dev, fw), BF16),
        pltpu.VMEM((tok_dev, fw), BF16),
        pltpu.VMEM((own_blocks, BLK, BLK), F32),
        pltpu.VMEM((own_blocks, BLK, BLK), F32),
    )
    operands = [
        pltpu.with_memory_space_constraint(array, pltpu.HBM)
        for array in (tokens, cotangent, w1_index.T, w2_index.T, w1_blocks, w2_blocks)
    ]
    return pl.pallas_call(
        functools.partial(kernel, n_row, n_col, tile_rows, n_blocks, own_blocks, tok_dev),
        out_shape=shapes,
        in_specs=[vmem, vmem, hbm, hbm, hbm, hbm],
        out_specs=[vmem] * 4,
        scratch_shapes=[
            pltpu.SMEM((2, n_blocks), jnp.int32),
            pltpu.SMEM((2, n_blocks), jnp.int32),
            pltpu.VMEM((n_blocks + 1, BLK, BLK), BF16),
            pltpu.VMEM((n_blocks + 1, BLK, BLK), BF16),
            pltpu.VMEM((n_row, fw, BLK), BF16),
            pltpu.VMEM((n_row, BLK, fw), BF16),
            pltpu.VMEM((2, n_col) + piece, BF16),
            pltpu.VMEM((2, toks, fw), BF16),
            pltpu.VMEM((fw, toks), BF16),
            pltpu.VMEM((2, 2, toks, BLK), F32),
            pltpu.VMEM((2, 2, half + 1, toks, BLK), BF16),
            pltpu.VMEM((toks, BLK), F32),
            pltpu.VMEM((n_row, toks, BLK), BF16),
            pltpu.VMEM((n_row, toks, BLK), BF16),
            pltpu.VMEM((2, toks, fw), F32),
            pltpu.VMEM((n_row, tile_rows, BLK, BLK), BF16),
            pltpu.VMEM((n_row, tile_rows, BLK, BLK), BF16),
            pltpu.VMEM((2, 2) + piece, F32),
            pltpu.VMEM((2,) + piece, F32),
            pltpu.VMEM((2, n_chip) + piece, BF16),
            pltpu.VMEM((2, n_chip) + piece, BF16),
            pltpu.VMEM((2, n_chip) + piece, BF16),
            pltpu.VMEM((2, max(n_x - 1, 1), 2) + piece, BF16),
            pltpu.VMEM((2,) + piece, BF16),
            pltpu.VMEM((2,) + piece, BF16),
            pltpu.VMEM((2, own_blocks, BLK, BLK), BF16),
            pltpu.VMEM((2, own_blocks, BLK, BLK), BF16),
            dma((4,)),
            dma((2, n_col)),
            dma((2, n_col)),
            dma((2, 2, half + 1, SUBS)),
            dma((2, 2, half, SUBS)),
            dma((2, 2, half, SUBS)),
            dma((2, 2, half, SUBS)),
            dma((2, n_x)),
            dma((2, n_x)),
            dma((2, max(n_x - 1, 1))),
            dma((2, max(n_x - 1, 1))),
            dma((2, 2)),
            dma((2, own_blocks)),
            dma((2, own_blocks)),
        ],
        compiler_params=pltpu.CompilerParams(
            collective_id=0, has_side_effects=True, vmem_limit_bytes=44 * 1024 * 1024
        ),
        name="ffn",
    )(*operands)


def solution(mesh):
    return jax.shard_map(
        functools.partial(shards, mesh.shape["row"], mesh.shape["col"]),
        mesh=mesh,
        in_specs=(
            P(("col", "rep"), "row"),
            P(("col", "rep"), "row"),
            P(("row", "col"), None, None),
            P(("row", "col"), None),
            P(("row", "col"), None, None),
            P(("row", "col"), None),
        ),
        out_specs=(
            P(("col", "rep"), "row"),
            P(("col", "rep"), "row"),
            P(("row", "col", "rep"), None, None),
            P(("row", "col", "rep"), None, None),
        ),
        check_vma=False,
    )
```

```python
import functools
import math

import jax
import jax.numpy as jnp
from jax import lax
from jax.experimental import pallas as pl
from jax.experimental.pallas import tpu as pltpu
from jax.sharding import PartitionSpec as P

BLK = 128
SUBS = 2
LAG = 2
F32 = jnp.float32
BF16 = jnp.bfloat16
NN = (((1,), (0,)), ((), ()))
NT = (((1,), (1,)), ((), ()))
TN = (((0,), (0,)), ((), ()))
C0 = math.sqrt(2.0 / math.pi)
C1 = 0.044715


def mm(left, right, dims):
    return lax.dot_general(left, right, dims, preferred_element_type=F32)


def stack_blocks(wide, parts):
    return jnp.concatenate([wide[:, a * BLK : (a + 1) * BLK] for a in range(parts)], axis=0)


def widen_blocks(tall, parts):
    rows = tall.shape[0] // parts
    return jnp.concatenate([tall[a * rows : (a + 1) * rows, :] for a in range(parts)], axis=1)


def kernel(
    n_row, n_col, tile_rows, n_blocks, own_blocks, tok_dev,
    tok_ref, cot_ref, idx1_hbm, idx2_hbm, w1_hbm, w2_hbm,
    out_ref, gt_ref, gw1_ref, gw2_ref,
    idx1, idx2, w1v, w2v, w1d, w2d, xrecv, xp, xt, part, rs, hid, ag0, ag1, acc, g1d, g2d,
    yown, ylast, ys1, yr1, ys2, yr2, ys3, yr3, wsend, wrecv,
    load_sem, x_send, x_recv, rs_send, rs_recv, ag_send, ag_recv, y1_send, y1_recv, y2_send, y2_recv, y3_sem, w_send, w_recv,
):
    ag = (ag0, ag1)
    z = lax.axis_index("row")
    c = lax.axis_index("col")
    p = lax.axis_index("rep")
    up, down = lax.rem(z + 1, n_row), lax.rem(z + n_row - 1, n_row)
    nxt = (up, down)
    half = n_row // 2
    tokens = tok_dev * n_col
    sub_rows = tokens // SUBS
    fw = tile_rows * BLK
    n_x = n_col // 4
    col_bits = n_col.bit_length() - 1
    bits = [lax.rem(c // (1 << b), 2) for b in range(col_bits)]
    core, y_hi = bits[0], bits[1]

    def flip(q):
        return sum((1 - bits[b] if (q >> b) & 1 else bits[b]) * (1 << b) for b in range(col_bits))

    own_place = 2 * (c // 4) + core

    loads = [
        pltpu.make_async_copy(idx1_hbm, idx1, load_sem.at[0]),
        pltpu.make_async_copy(idx2_hbm, idx2, load_sem.at[1]),
        pltpu.make_async_copy(w1_hbm, w1v.at[pl.ds(0, n_blocks)], load_sem.at[2]),
        pltpu.make_async_copy(w2_hbm, w2v.at[pl.ds(0, n_blocks)], load_sem.at[3]),
    ]
    for load in loads:
        load.start()

    barrier = pltpu.get_barrier_semaphore()
    peers = [flip(q) for q in range(1, n_col)]
    for peer in peers:
        pl.semaphore_signal(barrier, inc=1, device_id={"col": peer})
    pl.semaphore_signal(barrier, inc=1, device_id={"row": up})
    pl.semaphore_signal(barrier, inc=1, device_id={"row": down})
    pl.semaphore_signal(barrier, inc=1, device_id={"rep": 1 - p})

    for x, ref in enumerate((tok_ref, cot_ref)):
        xrecv[x, own_place] = stack_blocks(ref[...].astype(F32), tile_rows).astype(BF16)
    pl.semaphore_wait(barrier, len(peers) + 3)

    near = [q for q in range(1, n_col) if not q & 2]
    far = [q for q in range(1, n_col) if q & 2]
    even = [q for q in far + near if q % 2 == 0]

    def place(q):
        return (q >> 1 & 1) * (n_col // 2) + 2 * (flip(q) // 4) + (1 - core if q % 2 else core)

    def x_copy(x, q, direct=True):
        source = place(0) if direct else place(q)
        return pltpu.make_async_remote_copy(
            src_ref=xrecv.at[x, source],
            dst_ref=xrecv.at[x, (q >> 1 & 1) * (n_col // 2) + place(0) if direct else place(q)],
            send_sem=x_send.at[x, q],
            recv_sem=x_recv.at[x, q],
            device_id={"col": flip(q if x == 0 else (1 if q % 2 else q))},
        )

    def x_arrive(x, q):
        x_copy(x, q, False).wait_recv()

    def x_start(x):
        for q in even + [1] if x else near + far:
            x_copy(x, q).start()

    def x_forward(x):
        for q in reversed(even):
            x_arrive(x, q)
            pltpu.make_async_remote_copy(
                src_ref=xrecv.at[x, place(q)],
                dst_ref=xrecv.at[x, place(q)],
                send_sem=x_send.at[x, q + 1],
                recv_sem=x_recv.at[x, q + 1],
                device_id={"col": flip(1)},
            ).start()

    def panel(x, part_no):
        for q in (near, far)[part_no]:
            if x == 0 or q % 2:
                x_arrive(x, q)
        for m in range(n_col // 4):
            at = part_no * (n_col // 2) + 2 * m
            pair = [widen_blocks(xrecv[x, at + h].astype(F32), tile_rows) for h in range(2)]
            xp[x, pl.ds(at * tok_dev, 2 * tok_dev)] = jnp.concatenate(pair, axis=0).astype(BF16)

    x_start(0)

    zero_block = jnp.zeros((BLK, BLK), BF16)
    w1v[n_blocks] = zero_block
    w2v[n_blocks] = zero_block
    zeros_half = jnp.zeros((tokens // 2, BLK), BF16)
    for ph in range(2):
        for way in range(2):
            for s_half in range(2):
                is_long = (s_half == 0) == (way == 0)
                rs[ph, way, half if is_long else half - 1, pl.ds(s_half * (tokens // 2), tokens // 2)] = zeros_half

    def holder(keys, slot):
        found = jnp.int32(n_blocks)
        for n, key in enumerate(keys):
            found = jnp.where(key == slot, jnp.int32(n), found)
        return found

    def dense1():
        loads[0].wait()
        loads[2].wait()
        keys = [idx1[0, n] * n_row + idx1[1, n] for n in range(n_blocks)]

        def one(j, carry):
            for a in range(tile_rows):
                w1d[j, a * BLK : (a + 1) * BLK, :] = w1v[holder(keys, a * n_row + j)]
            return carry

        lax.fori_loop(0, n_row, one, 0)

    def dense2():
        loads[1].wait()
        loads[3].wait()
        keys = [idx2[0, n] * tile_rows + idx2[1, n] for n in range(n_blocks)]

        def one(j, carry):
            for a in range(tile_rows):
                w2d[j, :, a * BLK : (a + 1) * BLK] = w2v[holder(keys, j * tile_rows + a)]
            return carry

        lax.fori_loop(0, n_row, one, 0)

    def toward(way, d):
        return lax.rem(z + d, n_row) if way == 0 else lax.rem(z + n_row - d, n_row)

    def long_way(way, s):
        return (s < SUBS // 2) == (way == 0)

    def sub(s):
        return pl.ds(s * sub_rows, sub_rows)

    def product(ph, j, rows):
        if ph == 0:
            return mm(xp[0, rows], w1d[j], NN)
        return mm(xp[1, rows], w2d[j], NT)

    def rs_copy(ph, way, d, s):
        return pltpu.make_async_remote_copy(
            src_ref=rs.at[ph, way, d, sub(s)],
            dst_ref=rs.at[ph, way, d - 1, sub(s)],
            send_sem=rs_send.at[ph, way, d, s],
            recv_sem=rs_recv.at[ph, way, d - 1, s],
            device_id={"row": nxt[way]},
        )

    def rs_terms(ph, n, subs):
        for s in subs:
            for way in range(2):
                d = (half if long_way(way, s) else half - 1) - n

                @pl.when(d >= 1)
                def _(s=s, way=way, d=d):
                    part[ph, way, sub(s)] = product(ph, toward(way, d), sub(s))

    def rs_pass(ph, n, subs):
        for s in subs:
            for way in range(2):
                d = (half if long_way(way, s) else half - 1) - n

                @pl.when(d >= 1)
                def _(s=s, way=way, d=d):
                    @pl.when(n >= 1)
                    def _():
                        rs_copy(ph, way, d + 1, s).wait_recv()

                    total = part[ph, way, sub(s)] + rs[ph, way, d, sub(s)].astype(F32)
                    rs[ph, way, d, sub(s)] = total.astype(BF16)
                    rs_copy(ph, way, d, s).start()

    def rs_end(ph):
        for s in range(SUBS):
            part[ph, 0, sub(s)] = product(ph, z, sub(s))
        for s in range(SUBS):
            for way in range(2):
                rs_copy(ph, way, 1, s).wait_recv()
            total = part[ph, 0, sub(s)] + rs[ph, 0, 0, sub(s)].astype(F32) + rs[ph, 1, 0, sub(s)].astype(F32)
            if ph == 0:
                hid[sub(s)] = total
                tanh = jnp.tanh(C0 * (total + C1 * (total * total * total)))
                value = 0.5 * total * (1.0 + tanh)
            else:
                v = hid[sub(s)]
                tanh = jnp.tanh(C0 * (v + C1 * (v * v * v)))
                slope = 0.5 * (1.0 + tanh) + 0.5 * v * (1.0 - tanh * tanh) * (C0 * (1.0 + 3.0 * C1 * (v * v)))
                value = total * slope
            ag[ph][z, sub(s)] = value.astype(BF16)
            for way in range(2):
                ag_copy(ph, way, z, 0, s).start()

    def origin(way, t):
        return lax.rem(z + n_row - t, n_row) if way == 0 else lax.rem(z + t, n_row)

    def ag_copy(ph, way, j, t, s):
        return pltpu.make_async_remote_copy(
            src_ref=ag[ph].at[j, sub(s)],
            dst_ref=ag[ph].at[j, sub(s)],
            send_sem=ag_send.at[ph, way, t, s],
            recv_sem=ag_recv.at[ph, way, t, s],
            device_id={"row": nxt[way]},
        )

    def ag_pass(ph, t):
        for s in range(SUBS):
            for way in range(2):
                hops = half if long_way(way, s) else half - 1
                j = origin(way, t)

                @pl.when(t <= hops)
                def _(s=s, way=way, j=j):
                    ag_copy(ph, way, j, t - 1, s).wait_recv()

                @pl.when(t <= hops - 1)
                def _(s=s, way=way, j=j):
                    ag_copy(ph, way, j, t, s).start()

    def use_sum(ph, j):
        if ph == 0:
            acc[0] += mm(ag0[j], w2d[j], NN)
        else:
            acc[1] += mm(ag1[j], w1d[j], NT)

    def use_grad(ph, j):
        if ph == 0:
            grad = mm(ag0[j], xp[1], TN)
            for a in range(tile_rows):
                g2d[j, a] = grad[:, a * BLK : (a + 1) * BLK].astype(BF16)
        else:
            grad = mm(xt[...], ag1[j], NN)
            for a in range(tile_rows):
                g1d[j, a] = grad[a * BLK : (a + 1) * BLK, :].astype(BF16)

    def consume(ph, j):
        use_sum(ph, j)
        use_grad(ph, j)

    def ag_use(ph, t):
        consume(ph, origin(0, t))

        @pl.when((t >= 1) & (t <= half - 1))
        def _():
            consume(ph, origin(1, t))

    def item(i, phases):
        for ph in phases:
            n = i - LAG * ph

            @pl.when(n < half)
            def _(ph=ph, n=n):
                rs_terms(ph, n, range(SUBS))
                rs_pass(ph, n, range(SUBS))

            @pl.when(n == half)
            def _(ph=ph):
                rs_end(ph)

            @pl.when(n > half)
            def _(ph=ph, n=n):
                ag_pass(ph, n - half)

        for ph in phases:
            n = i - LAG * ph

            @pl.when((n >= half) & (n <= 2 * half))
            def _(ph=ph, n=n):
                ag_use(ph, n - half)

    def packed(ph, at):
        rows = acc[ph, pl.ds(pl.multiple_of(at * tok_dev, 8), tok_dev), :]
        return stack_blocks(rows, tile_rows)

    def y1_copy(ph, dx):
        at = 2 * (flip(4 * dx) // 4)
        return pltpu.make_async_remote_copy(
            src_ref=ys1.at[ph, pl.ds(at, 2)],
            dst_ref=yr1.at[ph, pl.ds(at, 2)],
            send_sem=y1_send.at[ph, dx],
            recv_sem=y1_recv.at[ph, dx],
            device_id={"col": flip(1)},
        )

    def y2_copy(ph, dx):
        to = flip(4 * dx)
        return pltpu.make_async_remote_copy(
            src_ref=ys2.at[ph, pl.ds(2 * (to // 4), 2)],
            dst_ref=yr2.at[ph, dx - 1],
            send_sem=y2_send.at[ph, dx - 1],
            recv_sem=y2_recv.at[ph, dx - 1],
            device_id={"col": to},
        )

    def y3_copy(ph):
        return pltpu.make_async_remote_copy(
            src_ref=ys3.at[ph],
            dst_ref=yr3.at[ph],
            send_sem=y3_sem.at[0, ph],
            recv_sem=y3_sem.at[1, ph],
            device_id={"col": flip(2)},
        )

    x_order = sorted(range(n_x), key=lambda dx: (dx == 0, dx != 2))

    def y1(ph):
        for dx in x_order:
            at = 2 * (flip(4 * dx) // 4)
            for y in range(2):
                ys1[ph, at + y] = packed(ph, lax.rem(y + y_hi, 2) * (n_col // 2) + at + 1 - core).astype(BF16)
            y1_copy(ph, dx).start()

    def y2(ph):
        for dx in x_order:
            at = 2 * (flip(4 * dx) // 4)
            own = [packed(ph, lax.rem(y + y_hi, 2) * (n_col // 2) + at + core) for y in range(2)]
            y1_copy(ph, dx).wait_recv()
            for y in range(2):
                total = own[y] + yr1[ph, at + y].astype(F32)
                if dx:
                    ys2[ph, at + y] = total.astype(BF16)
                else:
                    yown[ph, y] = total
            if dx:
                y2_copy(ph, dx).start()

    def y3(ph):
        for dx in range(1, n_x):
            y2_copy(ph, dx).wait_recv()

        def summed(at):
            total = yown[ph, at]
            for dx in range(1, n_x):
                total += yr2[ph, dx - 1, at].astype(F32)
            return total

        ys3[ph] = summed(1 - y_hi).astype(BF16)
        y3_copy(ph).start()
        ylast[ph] = summed(y_hi)

    def y4(ph, ref):
        y3_copy(ph).wait_recv()
        ref[...] = widen_blocks(ylast[ph] + yr3[ph].astype(F32), tile_rows).astype(BF16)

    def w_copy(ph, m):
        return pltpu.make_async_remote_copy(
            src_ref=wsend.at[ph, m],
            dst_ref=wrecv.at[ph, m],
            send_sem=w_send.at[ph, m],
            recv_sem=w_recv.at[ph, m],
            device_id={"rep": 1 - p},
        )

    def weight_block(ph, n):
        if ph == 0:
            return g2d[idx2[0, n], idx2[1, n]]
        return g1d[idx1[1, n], idx1[0, n]]

    def send_weights(ph):
        def one(m, carry):
            wsend[ph, m] = weight_block(ph, (1 - p) * own_blocks + m)
            w_copy(ph, m).start()
            return carry

        lax.fori_loop(0, own_blocks, one, 0)

    def sum_weights(ph, ref):
        def one(m, carry):
            w_copy(ph, m).wait_recv()
            ref[m] = weight_block(ph, p * own_blocks + m).astype(F32) + wrecv[ph, m].astype(F32)
            return carry

        lax.fori_loop(0, own_blocks, one, 0)

    def sent_gathers(ph):
        for way in range(2):
            for s in range(SUBS):

                def one(t, carry, way=way, s=s):
                    ag_copy(ph, way, z, t, s).wait_send()
                    return carry

                lax.fori_loop(0, half if long_way(way, s) else half - 1, one, 0)

    def sent_first():
        for ph in range(2):
            for q in range(1, n_col):
                x_copy(ph, q).wait_send()
            for way in range(2):
                for s in range(SUBS):

                    def one(t, carry, ph=ph, way=way, s=s):
                        rs_copy(ph, way, t + 1, s).wait_send()
                        return carry

                    lax.fori_loop(0, half if long_way(way, s) else half - 1, one, 0)
        sent_gathers(0)

    def sent_results(ph):
        for dx in range(n_x):
            y1_copy(ph, dx).wait_send()
        for dx in range(1, n_x):
            y2_copy(ph, dx).wait_send()
        y3_copy(ph).wait_send()

        def one(m, carry):
            w_copy(ph, m).wait_send()
            return carry

        lax.fori_loop(0, own_blocks, one, 0)

    dense1()
    x_start(1)
    for s in range(SUBS):
        panel(0, s)
        rs_terms(0, 0, (s,))
        rs_pass(0, 0, (s,))
    dense2()
    for ph in range(2):
        acc[ph] = jnp.zeros((tokens, fw), F32)

    def first(i, carry):
        item(i, (0,))
        return carry

    lax.fori_loop(1, LAG, first, 0)
    x_forward(1)
    xt[...] = jnp.transpose(xp[0])
    panel(1, 0)
    panel(1, 1)

    def both(i, carry):
        item(i, (0, 1))

        @pl.when(i == 2 * half)
        def _():
            y1(0)
            send_weights(0)

        return carry

    lax.fori_loop(LAG, 2 * half + LAG, both, 0)
    y2(0)
    sent_first()
    ag_pass(1, half)
    last_block = origin(0, half)
    use_sum(1, last_block)
    y1(1)
    use_grad(1, last_block)
    send_weights(1)
    sent_gathers(1)
    y3(0)
    y2(1)
    y4(0, out_ref)
    sum_weights(0, gw2_ref)
    sent_results(0)
    y3(1)
    sum_weights(1, gw1_ref)
    y4(1, gt_ref)
    sent_results(1)


def shards(n_row, n_col, tokens, cotangent, w1_blocks, w1_index, w2_blocks, w2_index):
    tok_dev, fw = tokens.shape
    tile_rows = fw // BLK
    n_blocks = w1_blocks.shape[0]
    own_blocks = n_blocks // 2
    half = n_row // 2
    toks = tok_dev * n_col
    n_chip = n_col // 2
    n_x = n_col // 4
    piece = (tok_dev * tile_rows, BLK)
    vmem = pl.BlockSpec(memory_space=pltpu.VMEM)
    hbm = pl.BlockSpec(memory_space=pltpu.HBM)
    dma = pltpu.SemaphoreType.DMA
    shapes = (
        pltpu.VMEM((tok_dev, fw), BF16),
        pltpu.VMEM((tok_dev, fw), BF16),
        pltpu.VMEM((own_blocks, BLK, BLK), F32),
        pltpu.VMEM((own_blocks, BLK, BLK), F32),
    )
    operands = [
        pltpu.with_memory_space_constraint(array, pltpu.HBM)
        for array in (tokens, cotangent, w1_index.T, w2_index.T, w1_blocks, w2_blocks)
    ]
    return pl.pallas_call(
        functools.partial(kernel, n_row, n_col, tile_rows, n_blocks, own_blocks, tok_dev),
        out_shape=shapes,
        in_specs=[vmem, vmem, hbm, hbm, hbm, hbm],
        out_specs=[vmem] * 4,
        scratch_shapes=[
            pltpu.SMEM((2, n_blocks), jnp.int32),
            pltpu.SMEM((2, n_blocks), jnp.int32),
            pltpu.VMEM((n_blocks + 1, BLK, BLK), BF16),
            pltpu.VMEM((n_blocks + 1, BLK, BLK), BF16),
            pltpu.VMEM((n_row, fw, BLK), BF16),
            pltpu.VMEM((n_row, BLK, fw), BF16),
            pltpu.VMEM((2, n_col) + piece, BF16),
            pltpu.VMEM((2, toks, fw), BF16),
            pltpu.VMEM((fw, toks), BF16),
            pltpu.VMEM((2, 2, toks, BLK), F32),
            pltpu.VMEM((2, 2, half + 1, toks, BLK), BF16),
            pltpu.VMEM((toks, BLK), F32),
            pltpu.VMEM((n_row, toks, BLK), BF16),
            pltpu.VMEM((n_row, toks, BLK), BF16),
            pltpu.VMEM((2, toks, fw), F32),
            pltpu.VMEM((n_row, tile_rows, BLK, BLK), BF16),
            pltpu.VMEM((n_row, tile_rows, BLK, BLK), BF16),
            pltpu.VMEM((2, 2) + piece, F32),
            pltpu.VMEM((2,) + piece, F32),
            pltpu.VMEM((2, n_chip) + piece, BF16),
            pltpu.VMEM((2, n_chip) + piece, BF16),
            pltpu.VMEM((2, n_chip) + piece, BF16),
            pltpu.VMEM((2, max(n_x - 1, 1), 2) + piece, BF16),
            pltpu.VMEM((2,) + piece, BF16),
            pltpu.VMEM((2,) + piece, BF16),
            pltpu.VMEM((2, own_blocks, BLK, BLK), BF16),
            pltpu.VMEM((2, own_blocks, BLK, BLK), BF16),
            dma((4,)),
            dma((2, n_col)),
            dma((2, n_col)),
            dma((2, 2, half + 1, SUBS)),
            dma((2, 2, half, SUBS)),
            dma((2, 2, half, SUBS)),
            dma((2, 2, half, SUBS)),
            dma((2, n_x)),
            dma((2, n_x)),
            dma((2, max(n_x - 1, 1))),
            dma((2, max(n_x - 1, 1))),
            dma((2, 2)),
            dma((2, own_blocks)),
            dma((2, own_blocks)),
        ],
        compiler_params=pltpu.CompilerParams(
            collective_id=0, has_side_effects=True, vmem_limit_bytes=44 * 1024 * 1024
        ),
        name="ffn",
    )(*operands)


def solution(mesh):
    return jax.shard_map(
        functools.partial(shards, mesh.shape["row"], mesh.shape["col"]),
        mesh=mesh,
        in_specs=(
            P(("col", "rep"), "row"),
            P(("col", "rep"), "row"),
            P(("row", "col"), None, None),
            P(("row", "col"), None),
            P(("row", "col"), None, None),
            P(("row", "col"), None),
        ),
        out_specs=(
            P(("col", "rep"), "row"),
            P(("col", "rep"), "row"),
            P(("row", "col", "rep"), None, None),
            P(("row", "col", "rep"), None, None),
        ),
        check_vma=False,
    )
```

```python
import functools
import math

import jax
import jax.numpy as jnp
from jax import lax
from jax.experimental import pallas as pl
from jax.experimental.pallas import tpu as pltpu
from jax.sharding import PartitionSpec as P

BLK = 128
SUBS = 2
LAG = 2
F32 = jnp.float32
BF16 = jnp.bfloat16
NN = (((1,), (0,)), ((), ()))
NT = (((1,), (1,)), ((), ()))
TN = (((0,), (0,)), ((), ()))
C0 = math.sqrt(2.0 / math.pi)
C1 = 0.044715


def mm(left, right, dims):
    return lax.dot_general(left, right, dims, preferred_element_type=F32)


def stack_blocks(wide, parts):
    return jnp.concatenate([wide[:, a * BLK : (a + 1) * BLK] for a in range(parts)], axis=0)


def widen_blocks(tall, parts):
    rows = tall.shape[0] // parts
    return jnp.concatenate([tall[a * rows : (a + 1) * rows, :] for a in range(parts)], axis=1)


def kernel(
    n_row, n_col, tile_rows, n_blocks, own_blocks, tok_dev,
    tok_ref, cot_ref, idx1_hbm, idx2_hbm, w1_hbm, w2_hbm,
    out_ref, gt_ref, gw1_ref, gw2_ref,
    idx1, idx2, w1v, w2v, w1d, w2d, xrecv, xp, xt, part, rs, hid, ag0, ag1, acc, g1d, g2d,
    yown, ylast, ys1, yr1, ys2, yr2, ys3, yr3, wsend, wrecv,
    load_sem, x_send, x_recv, rs_send, rs_recv, ag_send, ag_recv, y1_send, y1_recv, y2_send, y2_recv, y3_sem, w_send, w_recv,
):
    ag = (ag0, ag1)
    z = lax.axis_index("row")
    c = lax.axis_index("col")
    p = lax.axis_index("rep")
    up, down = lax.rem(z + 1, n_row), lax.rem(z + n_row - 1, n_row)
    nxt = (up, down)
    half = n_row // 2
    tokens = tok_dev * n_col
    sub_rows = tokens // SUBS
    fw = tile_rows * BLK
    n_x = n_col // 4
    col_bits = n_col.bit_length() - 1
    bits = [lax.rem(c // (1 << b), 2) for b in range(col_bits)]
    core, y_hi = bits[0], bits[1]

    def flip(q):
        return sum((1 - bits[b] if (q >> b) & 1 else bits[b]) * (1 << b) for b in range(col_bits))

    own_place = 2 * (c // 4) + core

    loads = [
        pltpu.make_async_copy(idx1_hbm, idx1, load_sem.at[0]),
        pltpu.make_async_copy(idx2_hbm, idx2, load_sem.at[1]),
        pltpu.make_async_copy(w1_hbm, w1v.at[pl.ds(0, n_blocks)], load_sem.at[2]),
        pltpu.make_async_copy(w2_hbm, w2v.at[pl.ds(0, n_blocks)], load_sem.at[3]),
    ]
    for load in loads:
        load.start()

    barrier = pltpu.get_barrier_semaphore()
    peers = [flip(q) for q in range(1, n_col)]
    for peer in peers:
        pl.semaphore_signal(barrier, inc=1, device_id={"col": peer})
    pl.semaphore_signal(barrier, inc=1, device_id={"row": up})
    pl.semaphore_signal(barrier, inc=1, device_id={"row": down})
    pl.semaphore_signal(barrier, inc=1, device_id={"rep": 1 - p})

    for x, ref in enumerate((tok_ref, cot_ref)):
        xrecv[x, own_place] = stack_blocks(ref[...].astype(F32), tile_rows).astype(BF16)
    pl.semaphore_wait(barrier, len(peers) + 3)

    near = [q for q in range(1, n_col) if not q & 2]
    far = [q for q in range(1, n_col) if q & 2]
    even = [q for q in far + near if q % 2 == 0]

    def place(q):
        return (q >> 1 & 1) * (n_col // 2) + 2 * (flip(q) // 4) + (1 - core if q % 2 else core)

    def x_copy(x, q, direct=True):
        source = place(0) if direct else place(q)
        return pltpu.make_async_remote_copy(
            src_ref=xrecv.at[x, source],
            dst_ref=xrecv.at[x, (q >> 1 & 1) * (n_col // 2) + place(0) if direct else place(q)],
            send_sem=x_send.at[x, q],
            recv_sem=x_recv.at[x, q],
            device_id={"col": flip(q if x == 0 else (1 if q % 2 else q))},
        )

    def x_arrive(x, q):
        x_copy(x, q, False).wait_recv()

    def x_start(x):
        for q in even + [1] if x else near + far:
            x_copy(x, q).start()

    def x_forward(x):
        for q in reversed(even):
            x_arrive(x, q)
            pltpu.make_async_remote_copy(
                src_ref=xrecv.at[x, place(q)],
                dst_ref=xrecv.at[x, place(q)],
                send_sem=x_send.at[x, q + 1],
                recv_sem=x_recv.at[x, q + 1],
                device_id={"col": flip(1)},
            ).start()

    def panel(x, part_no):
        for q in (near, far)[part_no]:
            if x == 0 or q % 2:
                x_arrive(x, q)
        for m in range(n_col // 4):
            at = part_no * (n_col // 2) + 2 * m
            pair = [widen_blocks(xrecv[x, at + h].astype(F32), tile_rows) for h in range(2)]
            xp[x, pl.ds(at * tok_dev, 2 * tok_dev)] = jnp.concatenate(pair, axis=0).astype(BF16)

    x_start(0)

    zero_block = jnp.zeros((BLK, BLK), BF16)
    w1v[n_blocks] = zero_block
    w2v[n_blocks] = zero_block
    zeros_half = jnp.zeros((tokens // 2, BLK), BF16)
    for ph in range(2):
        for way in range(2):
            for s_half in range(2):
                is_long = (s_half == 0) == (way == 0)
                rs[ph, way, half if is_long else half - 1, pl.ds(s_half * (tokens // 2), tokens // 2)] = zeros_half

    def holder(keys, slot):
        found = jnp.int32(n_blocks)
        for n, key in enumerate(keys):
            found = jnp.where(key == slot, jnp.int32(n), found)
        return found

    def dense1():
        loads[0].wait()
        loads[2].wait()
        keys = [idx1[0, n] * n_row + idx1[1, n] for n in range(n_blocks)]

        def one(j, carry):
            for a in range(tile_rows):
                w1d[j, a * BLK : (a + 1) * BLK, :] = w1v[holder(keys, a * n_row + j)]
            return carry

        lax.fori_loop(0, n_row, one, 0)

    def dense2():
        loads[1].wait()
        loads[3].wait()
        keys = [idx2[0, n] * tile_rows + idx2[1, n] for n in range(n_blocks)]

        def one(j, carry):
            for a in range(tile_rows):
                w2d[j, :, a * BLK : (a + 1) * BLK] = w2v[holder(keys, j * tile_rows + a)]
            return carry

        lax.fori_loop(0, n_row, one, 0)

    def toward(way, d):
        return lax.rem(z + d, n_row) if way == 0 else lax.rem(z + n_row - d, n_row)

    def long_way(way, s):
        return (s < SUBS // 2) == (way == 0)

    def sub(s):
        return pl.ds(s * sub_rows, sub_rows)

    def product(ph, j, rows):
        if ph == 0:
            return mm(xp[0, rows], w1d[j], NN)
        return mm(xp[1, rows], w2d[j], NT)

    def rs_copy(ph, way, d, s):
        return pltpu.make_async_remote_copy(
            src_ref=rs.at[ph, way, d, sub(s)],
            dst_ref=rs.at[ph, way, d - 1, sub(s)],
            send_sem=rs_send.at[ph, way, d, s],
            recv_sem=rs_recv.at[ph, way, d - 1, s],
            device_id={"row": nxt[way]},
        )

    def rs_terms(ph, n, subs):
        for s in subs:
            for way in range(2):
                d = (half if long_way(way, s) else half - 1) - n

                @pl.when(d >= 1)
                def _(s=s, way=way, d=d):
                    part[ph, way, sub(s)] = product(ph, toward(way, d), sub(s))

    def rs_pass(ph, n, subs):
        for s in subs:
            for way in range(2):
                d = (half if long_way(way, s) else half - 1) - n

                @pl.when(d >= 1)
                def _(s=s, way=way, d=d):
                    @pl.when(n >= 1)
                    def _():
                        rs_copy(ph, way, d + 1, s).wait_recv()

                    total = part[ph, way, sub(s)] + rs[ph, way, d, sub(s)].astype(F32)
                    rs[ph, way, d, sub(s)] = total.astype(BF16)
                    rs_copy(ph, way, d, s).start()

    def rs_end(ph):
        for s in range(SUBS):
            part[ph, 0, sub(s)] = product(ph, z, sub(s))
        for s in range(SUBS):
            for way in range(2):
                rs_copy(ph, way, 1, s).wait_recv()
            total = part[ph, 0, sub(s)] + rs[ph, 0, 0, sub(s)].astype(F32) + rs[ph, 1, 0, sub(s)].astype(F32)
            if ph == 0:
                hid[sub(s)] = total
                tanh = jnp.tanh(C0 * (total + C1 * (total * total * total)))
                value = 0.5 * total * (1.0 + tanh)
            else:
                value = total * hid[sub(s)]
            ag[ph][z, sub(s)] = value.astype(BF16)
            for way in range(2):
                ag_copy(ph, way, z, 0, s).start()
        if ph == 0:
            for s in range(SUBS):
                v = hid[sub(s)]
                tanh = jnp.tanh(C0 * (v + C1 * (v * v * v)))
                slope = 0.5 * (1.0 + tanh) + 0.5 * v * (1.0 - tanh * tanh) * (C0 * (1.0 + 3.0 * C1 * (v * v)))
                hid[sub(s)] = slope

    def origin(way, t):
        return lax.rem(z + n_row - t, n_row) if way == 0 else lax.rem(z + t, n_row)

    def ag_copy(ph, way, j, t, s):
        return pltpu.make_async_remote_copy(
            src_ref=ag[ph].at[j, sub(s)],
            dst_ref=ag[ph].at[j, sub(s)],
            send_sem=ag_send.at[ph, way, t, s],
            recv_sem=ag_recv.at[ph, way, t, s],
            device_id={"row": nxt[way]},
        )

    def ag_pass(ph, t):
        for s in range(SUBS):
            for way in range(2):
                hops = half if long_way(way, s) else half - 1
                j = origin(way, t)

                @pl.when(t <= hops)
                def _(s=s, way=way, j=j):
                    ag_copy(ph, way, j, t - 1, s).wait_recv()

                @pl.when(t <= hops - 1)
                def _(s=s, way=way, j=j):
                    ag_copy(ph, way, j, t, s).start()

    def use_sum(ph, j):
        if ph == 0:
            acc[0] += mm(ag0[j], w2d[j], NN)
        else:
            acc[1] += mm(ag1[j], w1d[j], NT)

    def use_grad(ph, j):
        if ph == 0:
            grad = mm(ag0[j], xp[1], TN)
            for a in range(tile_rows):
                g2d[j, a] = grad[:, a * BLK : (a + 1) * BLK].astype(BF16)
        else:
            grad = mm(xt[...], ag1[j], NN)
            for a in range(tile_rows):
                g1d[j, a] = grad[a * BLK : (a + 1) * BLK, :].astype(BF16)

    def consume(ph, j):
        use_sum(ph, j)
        use_grad(ph, j)

    def ag_use(ph, t):
        consume(ph, origin(0, t))

        @pl.when((t >= 1) & (t <= half - 1))
        def _():
            consume(ph, origin(1, t))

    def item(i, phases):
        for ph in phases:
            n = i - LAG * ph

            @pl.when(n < half)
            def _(ph=ph, n=n):
                rs_terms(ph, n, range(SUBS))
                rs_pass(ph, n, range(SUBS))

            @pl.when(n == half)
            def _(ph=ph):
                rs_end(ph)

            @pl.when(n > half)
            def _(ph=ph, n=n):
                ag_pass(ph, n - half)

        for ph in phases:
            n = i - LAG * ph

            @pl.when((n >= half) & (n <= 2 * half))
            def _(ph=ph, n=n):
                ag_use(ph, n - half)

    def packed(ph, at):
        rows = acc[ph, pl.ds(pl.multiple_of(at * tok_dev, 8), tok_dev), :]
        return stack_blocks(rows, tile_rows)

    def y1_copy(ph, dx):
        at = 2 * (flip(4 * dx) // 4)
        return pltpu.make_async_remote_copy(
            src_ref=ys1.at[ph, pl.ds(at, 2)],
            dst_ref=yr1.at[ph, pl.ds(at, 2)],
            send_sem=y1_send.at[ph, dx],
            recv_sem=y1_recv.at[ph, dx],
            device_id={"col": flip(1)},
        )

    def y2_copy(ph, dx):
        to = flip(4 * dx)
        return pltpu.make_async_remote_copy(
            src_ref=ys2.at[ph, pl.ds(2 * (to // 4), 2)],
            dst_ref=yr2.at[ph, dx - 1],
            send_sem=y2_send.at[ph, dx - 1],
            recv_sem=y2_recv.at[ph, dx - 1],
            device_id={"col": to},
        )

    def y3_copy(ph):
        return pltpu.make_async_remote_copy(
            src_ref=ys3.at[ph],
            dst_ref=yr3.at[ph],
            send_sem=y3_sem.at[0, ph],
            recv_sem=y3_sem.at[1, ph],
            device_id={"col": flip(2)},
        )

    x_order = sorted(range(n_x), key=lambda dx: (dx == 0, dx != 2))

    def y1(ph):
        for dx in x_order:
            at = 2 * (flip(4 * dx) // 4)
            for y in range(2):
                ys1[ph, at + y] = packed(ph, lax.rem(y + y_hi, 2) * (n_col // 2) + at + 1 - core).astype(BF16)
            y1_copy(ph, dx).start()

    def y2(ph):
        for dx in x_order:
            at = 2 * (flip(4 * dx) // 4)
            own = [packed(ph, lax.rem(y + y_hi, 2) * (n_col // 2) + at + core) for y in range(2)]
            y1_copy(ph, dx).wait_recv()
            for y in range(2):
                total = own[y] + yr1[ph, at + y].astype(F32)
                if dx:
                    ys2[ph, at + y] = total.astype(BF16)
                else:
                    yown[ph, y] = total
            if dx:
                y2_copy(ph, dx).start()

    def y3(ph):
        for dx in range(1, n_x):
            y2_copy(ph, dx).wait_recv()

        def summed(at):
            total = yown[ph, at]
            for dx in range(1, n_x):
                total += yr2[ph, dx - 1, at].astype(F32)
            return total

        ys3[ph] = summed(1 - y_hi).astype(BF16)
        y3_copy(ph).start()
        ylast[ph] = summed(y_hi)

    def y4(ph, ref):
        y3_copy(ph).wait_recv()
        ref[...] = widen_blocks(ylast[ph] + yr3[ph].astype(F32), tile_rows).astype(BF16)

    def w_copy(ph, m):
        return pltpu.make_async_remote_copy(
            src_ref=wsend.at[ph, m],
            dst_ref=wrecv.at[ph, m],
            send_sem=w_send.at[ph, m],
            recv_sem=w_recv.at[ph, m],
            device_id={"rep": 1 - p},
        )

    def weight_block(ph, n):
        if ph == 0:
            return g2d[idx2[0, n], idx2[1, n]]
        return g1d[idx1[1, n], idx1[0, n]]

    def send_weights(ph):
        def one(m, carry):
            wsend[ph, m] = weight_block(ph, (1 - p) * own_blocks + m)
            w_copy(ph, m).start()
            return carry

        lax.fori_loop(0, own_blocks, one, 0)

    def sum_weights(ph, ref):
        def one(m, carry):
            w_copy(ph, m).wait_recv()
            ref[m] = weight_block(ph, p * own_blocks + m).astype(F32) + wrecv[ph, m].astype(F32)
            return carry

        lax.fori_loop(0, own_blocks, one, 0)

    def sent_gathers(ph):
        for way in range(2):
            for s in range(SUBS):

                def one(t, carry, way=way, s=s):
                    ag_copy(ph, way, z, t, s).wait_send()
                    return carry

                lax.fori_loop(0, half if long_way(way, s) else half - 1, one, 0)

    def sent_first():
        for ph in range(2):
            for q in range(1, n_col):
                x_copy(ph, q).wait_send()
            for way in range(2):
                for s in range(SUBS):

                    def one(t, carry, ph=ph, way=way, s=s):
                        rs_copy(ph, way, t + 1, s).wait_send()
                        return carry

                    lax.fori_loop(0, half if long_way(way, s) else half - 1, one, 0)
        sent_gathers(0)

    def sent_results(ph):
        for dx in range(n_x):
            y1_copy(ph, dx).wait_send()
        for dx in range(1, n_x):
            y2_copy(ph, dx).wait_send()
        y3_copy(ph).wait_send()

        def one(m, carry):
            w_copy(ph, m).wait_send()
            return carry

        lax.fori_loop(0, own_blocks, one, 0)

    dense1()
    x_start(1)
    for s in range(SUBS):
        panel(0, s)
        rs_terms(0, 0, (s,))
        rs_pass(0, 0, (s,))
    dense2()
    for ph in range(2):
        acc[ph] = jnp.zeros((tokens, fw), F32)

    def first(i, carry):
        item(i, (0,))
        return carry

    lax.fori_loop(1, LAG, first, 0)
    x_forward(1)
    xt[...] = jnp.transpose(xp[0])
    panel(1, 0)
    panel(1, 1)

    def both(i, carry):
        item(i, (0, 1))

        @pl.when(i == 2 * half)
        def _():
            y1(0)
            send_weights(0)

        return carry

    lax.fori_loop(LAG, 2 * half + LAG, both, 0)
    y2(0)
    sent_first()
    ag_pass(1, half)
    last_block = origin(0, half)
    use_sum(1, last_block)
    y1(1)
    use_grad(1, last_block)
    send_weights(1)
    sent_gathers(1)
    y3(0)
    y2(1)
    y4(0, out_ref)
    sum_weights(0, gw2_ref)
    sent_results(0)
    y3(1)
    sum_weights(1, gw1_ref)
    y4(1, gt_ref)
    sent_results(1)


def shards(n_row, n_col, tokens, cotangent, w1_blocks, w1_index, w2_blocks, w2_index):
    tok_dev, fw = tokens.shape
    tile_rows = fw // BLK
    n_blocks = w1_blocks.shape[0]
    own_blocks = n_blocks // 2
    half = n_row // 2
    toks = tok_dev * n_col
    n_chip = n_col // 2
    n_x = n_col // 4
    piece = (tok_dev * tile_rows, BLK)
    vmem = pl.BlockSpec(memory_space=pltpu.VMEM)
    hbm = pl.BlockSpec(memory_space=pltpu.HBM)
    dma = pltpu.SemaphoreType.DMA
    shapes = (
        pltpu.VMEM((tok_dev, fw), BF16),
        pltpu.VMEM((tok_dev, fw), BF16),
        pltpu.VMEM((own_blocks, BLK, BLK), F32),
        pltpu.VMEM((own_blocks, BLK, BLK), F32),
    )
    operands = [
        pltpu.with_memory_space_constraint(array, pltpu.HBM)
        for array in (tokens, cotangent, w1_index.T, w2_index.T, w1_blocks, w2_blocks)
    ]
    return pl.pallas_call(
        functools.partial(kernel, n_row, n_col, tile_rows, n_blocks, own_blocks, tok_dev),
        out_shape=shapes,
        in_specs=[vmem, vmem, hbm, hbm, hbm, hbm],
        out_specs=[vmem] * 4,
        scratch_shapes=[
            pltpu.SMEM((2, n_blocks), jnp.int32),
            pltpu.SMEM((2, n_blocks), jnp.int32),
            pltpu.VMEM((n_blocks + 1, BLK, BLK), BF16),
            pltpu.VMEM((n_blocks + 1, BLK, BLK), BF16),
            pltpu.VMEM((n_row, fw, BLK), BF16),
            pltpu.VMEM((n_row, BLK, fw), BF16),
            pltpu.VMEM((2, n_col) + piece, BF16),
            pltpu.VMEM((2, toks, fw), BF16),
            pltpu.VMEM((fw, toks), BF16),
            pltpu.VMEM((2, 2, toks, BLK), F32),
            pltpu.VMEM((2, 2, half + 1, toks, BLK), BF16),
            pltpu.VMEM((toks, BLK), F32),
            pltpu.VMEM((n_row, toks, BLK), BF16),
            pltpu.VMEM((n_row, toks, BLK), BF16),
            pltpu.VMEM((2, toks, fw), F32),
            pltpu.VMEM((n_row, tile_rows, BLK, BLK), BF16),
            pltpu.VMEM((n_row, tile_rows, BLK, BLK), BF16),
            pltpu.VMEM((2, 2) + piece, F32),
            pltpu.VMEM((2,) + piece, F32),
            pltpu.VMEM((2, n_chip) + piece, BF16),
            pltpu.VMEM((2, n_chip) + piece, BF16),
            pltpu.VMEM((2, n_chip) + piece, BF16),
            pltpu.VMEM((2, max(n_x - 1, 1), 2) + piece, BF16),
            pltpu.VMEM((2,) + piece, BF16),
            pltpu.VMEM((2,) + piece, BF16),
            pltpu.VMEM((2, own_blocks, BLK, BLK), BF16),
            pltpu.VMEM((2, own_blocks, BLK, BLK), BF16),
            dma((4,)),
            dma((2, n_col)),
            dma((2, n_col)),
            dma((2, 2, half + 1, SUBS)),
            dma((2, 2, half, SUBS)),
            dma((2, 2, half, SUBS)),
            dma((2, 2, half, SUBS)),
            dma((2, n_x)),
            dma((2, n_x)),
            dma((2, max(n_x - 1, 1))),
            dma((2, max(n_x - 1, 1))),
            dma((2, 2)),
            dma((2, own_blocks)),
            dma((2, own_blocks)),
        ],
        compiler_params=pltpu.CompilerParams(
            collective_id=0, has_side_effects=True, vmem_limit_bytes=44 * 1024 * 1024
        ),
        name="ffn",
    )(*operands)


def solution(mesh):
    return jax.shard_map(
        functools.partial(shards, mesh.shape["row"], mesh.shape["col"]),
        mesh=mesh,
        in_specs=(
            P(("col", "rep"), "row"),
            P(("col", "rep"), "row"),
            P(("row", "col"), None, None),
            P(("row", "col"), None),
            P(("row", "col"), None, None),
            P(("row", "col"), None),
        ),
        out_specs=(
            P(("col", "rep"), "row"),
            P(("col", "rep"), "row"),
            P(("row", "col", "rep"), None, None),
            P(("row", "col", "rep"), None, None),
        ),
        check_vma=False,
    )
```
